32 devices in a mesh: rep: 2 (over y), fsdp: 8 (over z, x), seq: 2 (over core).
Axes of the slice: x: 2, y: 2, z: 4, core: 2. Of those that a mesh axis runs over, the one named last changes fastest.
Arguments:
- queries: bfloat16 [16, 256, 1536], P(('rep', 'fsdp'), 'seq'), parts along dimension 0, may hold values from -6 to 6
- image_keys: bfloat16 [16, 256, 1536], P(('rep', 'fsdp'), 'seq'), parts along dimension 0, may hold values from -6 to 6
- image_values: bfloat16 [16, 256, 1536], P(('rep', 'fsdp'), 'seq'), parts along dimension 0, may hold values from -6 to 6
- text_keys: bfloat16 [16, 128, 1536], P(('rep', 'fsdp')), parts along dimension 0, may hold values from -6 to 6
- text_values: bfloat16 [16, 128, 1536], P(('rep', 'fsdp')), parts along dimension 0, may hold values from -6 to 6
- control_hint: bfloat16 [16, 256, 128], P(('rep', 'fsdp'), 'seq'), parts along dimension 0, may hold values from -6 to 6
- proj_out: bfloat16 [1536, 3072], P('fsdp', 'seq'), may hold values from -0.15625 to 0.15625
- adapter_down: bfloat16 [1536, 128], P('fsdp'), may hold values from -0.15625 to 0.15625
- adapter_up: bfloat16 [128, 3072], P(None, 'fsdp'), may hold values from -0.5 to 0.5
- cotangent: bfloat16 [16, 256, 3072], P(('rep', 'fsdp'), 'seq'), parts along dimension 0, may hold values from -6 to 6
Outputs:
- update: bfloat16 [16, 256, 3072], P(('rep', 'fsdp'), 'seq'), parts along dimension 0
- query_grad: bfloat16 [16, 256, 1536], P(('rep', 'fsdp'), 'seq'), parts along dimension 0
- key_grad: bfloat16 [16, 256, 1536], P(('rep', 'fsdp'), 'seq'), parts along dimension 0
- value_grad: bfloat16 [16, 256, 1536], P(('rep', 'fsdp'), 'seq'), parts along dimension 0
- down_grad: float32 [3072, 128], P(('rep', 'fsdp', 'seq')), parts along dimension 0
- up_grad: float32 [256, 3072], P('rep', ('fsdp', 'seq')), parts along dimension 0
The draws below stay inside these ranges and needn't reach their ends.
There are 2 independent parts, one for each index of `rep`. The reference program is written for one: setup_inputs(seed, part) draws one part's arguments, and reference() takes and returns one part's arrays. A program takes and returns all parts, laid end to end along the dimension named above; an argument that names none is the same for every part. Nothing has to cross between parts.
All inputs are finite; a program needn't handle non-finite values.
Results may differ from the reference program's by a relative error of at most 0.011.
Values may be sent and summed in bfloat16 or wider, within the bound.
No kernel may reach another device: no remote copies, remote signals or barrier semaphores. Data moves between devices by JAX's collectives and lax.ppermute only.
A program may use at most 128 MiB of HBM per device.

```python
import math
import jax
import jax.numpy as jnp
from jax import lax

D = 3072
HD = 128
R = 128
TXT = 128
HW = 1536
SAMPLES = 8
IMG = 256


def draw_queries(key, part):
    key = jax.random.fold_in(key, 3)
    parts = jax.random.split(key, 2)
    scales = jnp.exp(jax.random.uniform(parts[1], (SAMPLES, IMG, 1), jnp.float32, math.log(0.3), math.log(1.2)))
    entries = jax.random.normal(parts[0], (SAMPLES, IMG, HW), jnp.float32)
    table = jnp.clip(entries * scales, -6.0, 6.0)
    return table.astype(jnp.bfloat16)


def draw_image_keys(key, part):
    key = jax.random.fold_in(key, 5)
    parts = jax.random.split(key, 2)
    scales = jnp.exp(jax.random.uniform(parts[1], (SAMPLES, IMG, 1), jnp.float32, math.log(0.3), math.log(3.0)))
    entries = jax.random.normal(parts[0], (SAMPLES, IMG, HW), jnp.float32)
    table = jnp.clip(entries * scales, -6.0, 6.0)
    return table.astype(jnp.bfloat16)


def strengthened(result, own_key, source, target, shards_of, factor):
    def block_of(position):
        return (jnp.arange(result.shape[position]) // (result.shape[position] // shards_of)).reshape((-1,) + (1,) * (result.ndim - 1 - position))

    near = jax.random.permutation(own_key, shards_of)[block_of(target)]
    other_side = (block_of(target) + shards_of // 2) % shards_of
    return jnp.where((block_of(source) == near) | (block_of(source) == other_side), factor * result, result)


def level_of(rng, extent, pieces, low, high):
    level, own = 1.0, jax.random.fold_in(rng, 6)
    for position, shards_of in pieces:
        steps = jnp.exp(jax.random.uniform(jax.random.fold_in(own, position), (shards_of,), jnp.float32, low / len(pieces), high / len(pieces)))
        level = level * jnp.repeat(steps, extent[position] // shards_of).reshape([-1 if axis == position else 1 for axis in range(len(extent))])
    return level


def centred(stream_key, extent, scale, limit, cuts=(), kind=jnp.bfloat16):
    drawn = jax.random.normal(stream_key, extent, jnp.float32) * scale
    if len(cuts) > 0:
        drawn = level_of(stream_key, extent, cuts, -0.22, 0.18) * drawn
    return jnp.clip(drawn, min=-limit, max=limit).astype(kind)


def bell_draw_with(own_key, extent, width, bound, shards, heavy, kind=jnp.bfloat16):
    values = width * jax.random.normal(own_key, extent, jnp.float32)
    if shards:
        values = values * level_of(own_key, extent, shards, -0.22, 0.18)
    return jnp.clip(strengthened(values, jax.random.fold_in(own_key, 3), *heavy), -bound, bound).astype(kind)


def setup_inputs(seed: int = 0, part: int = 0) -> dict:
    streams_of = jax.random.split(jax.random.key(seed), 11)
    own_keys = jax.random.split(jax.random.fold_in(streams_of[10], part), 11)
    return {
        "queries": draw_queries(jax.random.fold_in(jax.random.fold_in(streams_of[10], part), 71), part),
        "image_keys": draw_image_keys(jax.random.fold_in(jax.random.fold_in(streams_of[10], part), 71), part),
        "image_values": centred(own_keys[2], (SAMPLES, IMG, HW), 1.0, 6.0, ((0, 8), (1, 2))),
        "text_keys": centred(own_keys[3], (SAMPLES, TXT, HW), 1.0, 6.0, ((0, 8),)),
        "text_values": centred(own_keys[4], (SAMPLES, TXT, HW), 1.0, 6.0, ((0, 8),)),
        "control_hint": centred(own_keys[5], (SAMPLES, IMG, R), 1.0, 6.0, ((0, 8), (1, 2))),
        "proj_out": centred(streams_of[6], (HW, D), HW ** -0.5, 0.15625, ((0, 8), (1, 2))),
        "adapter_down": centred(streams_of[7], (HW, R), HW ** -0.5, 0.15625, ((0, 8),)),
        "adapter_up": centred(streams_of[8], (R, D), R ** -0.5, 0.5, ((1, 8),)),
        "cotangent": bell_draw_with(own_keys[9], (SAMPLES, IMG, D), 1.0, 6.0, ((0, 8), (1, 2)), (0, 2, 8, 2.0)),
    }


def split_heads(matrix):
    return matrix.astype(jnp.float32).reshape(matrix.shape[0], matrix.shape[1] // HD, HD)

def reference(queries, image_keys, image_values, text_keys, text_values, control_hint, proj_out, adapter_down, adapter_up, cotangent):
    factor = HD ** (-0.5)

    def sample_pass(totals, sample):
        q_rows, k_rows, v_rows, tk_rows, tv_rows, hint_rows, cot_rows = sample
        all_keys = jnp.concatenate([k_rows, tk_rows], 0)
        all_values = jnp.concatenate([v_rows, tv_rows], 0)
        q_heads = split_heads(q_rows)
        k_heads = split_heads(all_keys)
        v_heads = split_heads(all_values)
        scores = jnp.einsum('qhd,khd->hqk', q_heads, k_heads) * factor
        row_max = lax.optimization_barrier(jnp.max(scores, -1, keepdims=True))
        log_total = row_max + jnp.log(lax.optimization_barrier(jnp.sum(jnp.exp(scores - row_max), -1, keepdims=True)))
        attn_prob = jnp.exp(scores - log_total)
        prob_half = lax.optimization_barrier(attn_prob.astype(jnp.bfloat16)).astype(jnp.float32)
        attn = jnp.einsum('hqk,khd->qhd', prob_half, v_heads).reshape(IMG, HW).astype(jnp.bfloat16)
        pre_act = jnp.dot(attn, adapter_down, preferred_element_type=jnp.float32) + hint_rows.astype(jnp.float32)
        logistic = jax.nn.sigmoid(pre_act)
        adapter_act = (pre_act * logistic).astype(jnp.bfloat16)
        update = (jnp.dot(attn, proj_out, preferred_element_type=jnp.float32) + jnp.dot(adapter_act, adapter_up, preferred_element_type=jnp.float32)).astype(jnp.bfloat16)
        act_back = jnp.dot(cot_rows, adapter_up.T, preferred_element_type=jnp.float32)
        act_grad = (act_back * logistic * (1.0 + pre_act * (1.0 - logistic))).astype(jnp.bfloat16)
        attn_grad = (jnp.dot(cot_rows, proj_out.T, preferred_element_type=jnp.float32) + jnp.dot(act_grad, adapter_down.T, preferred_element_type=jnp.float32)).astype(jnp.bfloat16)
        down_total = totals[0] + jnp.dot(attn.T, act_grad, preferred_element_type=jnp.float32)
        up_total = totals[1] + jnp.dot(adapter_act.T, cot_rows, preferred_element_type=jnp.float32)
        grad_heads = split_heads(attn_grad)
        attn_heads = split_heads(attn)
        delta = jnp.einsum('qhd,qhd->hq', grad_heads, attn_heads)[:, :, None]
        prob_grad = jnp.einsum('qhd,khd->hqk', grad_heads, v_heads)
        score_grad = lax.optimization_barrier((attn_prob * (prob_grad - delta)).astype(jnp.bfloat16)).astype(jnp.float32)
        query_grad = (jnp.einsum('hqk,khd->qhd', score_grad, k_heads) * factor).reshape(IMG, HW).astype(jnp.bfloat16)
        key_grad = (jnp.einsum('hqk,qhd->khd', score_grad[:, :, :IMG], q_heads) * factor).reshape(IMG, HW).astype(jnp.bfloat16)
        value_grad = jnp.einsum('hqk,qhd->khd', prob_half[:, :, :IMG], grad_heads).reshape(IMG, HW).astype(jnp.bfloat16)
        return ((down_total, up_total), (update, query_grad, key_grad, value_grad))
    start = (jnp.zeros((HW, R), jnp.float32), jnp.zeros((R, D), jnp.float32))
    totals, outputs = lax.scan(sample_pass, start, (queries, image_keys, image_values, text_keys, text_values, control_hint, cotangent))
    grad_scale = 1.0 / math.sqrt(SAMPLES * IMG)
    return (outputs[0], outputs[1], outputs[2], outputs[3], totals[0] * grad_scale, totals[1] * grad_scale)
```

```python
import functools

import jax
import jax.numpy as jnp
from jax import lax
from jax.experimental import pallas as pl
from jax.experimental.pallas import tpu as pltpu
from jax.sharding import PartitionSpec as P

HD = 128
BATCHES = 4
ORDER = (0, 2, 4, 6, 1, 3, 5, 7)
FACTOR = HD ** (-0.5)
F32 = jnp.float32
BF16 = jnp.bfloat16
ROWS = (((0,), (0,)), ((), ()))
COLS = (((1,), (1,)), ((), ()))


def swap(value, axis, mask):
    pairs = [(source, source ^ mask) for source in range(lax.axis_size(axis))]
    return lax.ppermute(value, axis, pairs)


def ring_after(z):
    low, high = z % 2, z // 2
    return 2 * low + (1 - high)


def ring_before(z):
    low, high = z % 2, z // 2
    return 2 * (1 - low) + high


def ring_step(value):
    pairs = []
    for f in range(8):
        z, x = f // 2, f % 2
        pairs.append((f, ring_after(z) * 2 + x))
        pairs.append((8 + f, 8 + ring_before(z) * 2 + x))
    return lax.ppermute(value, ("rep", "fsdp"), pairs)


def dot(a, b, dims=None):
    if dims is None:
        return jnp.dot(a, b, preferred_element_type=F32)
    return lax.dot_general(a, b, dims, preferred_element_type=F32)


def batch_places(grouped):
    if not grouped:
        return list(range(BATCHES)), 0
    f = lax.axis_index("fsdp")
    rep = lax.axis_index("rep")
    z, x = f // 2, f % 2
    after, before = ring_after(z), ring_before(z)
    first = jnp.where(rep == 0, before, after)
    second = jnp.where(rep == 0, after, before)
    return [z, first, second, 3 - z], x


def softmax_parts(q, k):
    scores = dot(q, k, COLS) * FACTOR
    top = jnp.max(scores, -1, keepdims=True)
    weight = jnp.exp(scores - top)
    return weight * (1.0 / jnp.sum(weight, -1, keepdims=True))


def start_all(copies):
    for copy in copies:
        copy.start()


def forward_kernel(q, ko, kf, kt, vo, vf, vt, attn, keys, values, sems):
    rows, inner = q.shape
    copies = [
        pltpu.make_async_copy(source, target.at[pl.ds(i * rows, rows)], sems.at[j, i])
        for j, (sources, target) in enumerate((((ko, kf, kt), keys), ((vo, vf, vt), values)))
        for i, source in enumerate(sources)
    ]
    start_all(copies)
    for copy in copies:
        copy.wait()
    for h in range(inner // HD):
        c = slice(h * HD, (h + 1) * HD)
        prob = softmax_parts(q[:, c], keys[:, c]).astype(BF16)
        attn[:, c] = dot(prob, values[:, c]).astype(BF16)


def adapter_kernel(packed, scale, *refs):
    if packed:
        (mine, theirs, attn, cot, hint, down, up, act, act_grad, near, far, terms, sems) = refs
        f = lax.axis_index("fsdp")
        core = lax.axis_index("seq")
        copies = []
        for side, source in enumerate((mine, theirs)):
            half = core if side == 0 else 1 - core
            for place, mask in enumerate(ORDER):
                block = f ^ mask
                copies.append(
                    pltpu.make_async_copy(
                        source.at[place, pl.ds(0, 96)],
                        down.at[pl.ds(pl.multiple_of(block * 192 + half * 96, 32), 96)],
                        sems.at[len(copies)],
                    )
                )
                for j in range(3):
                    copies.append(
                        pltpu.make_async_copy(
                            source.at[place, pl.ds(96 + 64 * j, 64)],
                            up.at[
                                pl.ds(pl.multiple_of(half * 64, 64), 64),
                                pl.ds(pl.multiple_of(block * 384 + 128 * j, 128), 128),
                            ],
                            sems.at[len(copies)],
                        )
                    )
    else:
        (down_in, up_in, attn, cot, hint, down, up, act, act_grad, down_term, up_term, sems) = refs
        copies = [
            pltpu.make_async_copy(down_in, down, sems.at[0]),
            pltpu.make_async_copy(up_in, up, sems.at[1]),
        ]
    start_all(copies)
    for copy in copies:
        copy.wait()
    pre_act = dot(attn[...], down[...]) + hint[...].astype(F32)
    logistic = 1.0 / (1.0 + jnp.exp(-pre_act))
    act[...] = (pre_act * logistic).astype(BF16)
    act_back = dot(cot[...], up[...], COLS)
    act_grad[...] = (act_back * logistic * (1.0 + pre_act * (1.0 - logistic))).astype(BF16)
    inner, wide = attn.shape[1], cot.shape[1]
    if not packed:
        down_term[...] = dot(attn[...], act_grad[...], ROWS) * scale
        up_term[...] = dot(cot[...], act[...], ROWS) * scale
        return
    terms[pl.ds(0, inner)] = dot(attn[...], act_grad[...], ROWS) * scale
    terms[pl.ds(inner, wide)] = dot(cot[...], act[...], ROWS) * scale
    for place, mask in enumerate(ORDER):
        block = f ^ mask
        for target, half in ((near, core), (far, 1 - core)):
            piece = block * 2 + half
            target[place, 0:96] = terms[pl.ds(pl.multiple_of(piece * 96, 32), 96)]
            target[place, 96:288] = terms[pl.ds(pl.multiple_of(inner + piece * 192, 64), 192)]


def project_kernel(grouped, numbers, last, *refs):
    count = len(numbers)
    pieces = refs[: 2 * count]
    attn_own, attn_far, cot, cot_far = refs[2 * count : 2 * count + 4]
    rest = refs[2 * count + 4 :]
    total_in = None
    if numbers[0] > 0:
        total_in, rest = rest[0], rest[1:]
    if last:
        near, far, own, away, weights, sems = rest
    else:
        near, far, total, weights, sems = rest
    places, x = batch_places(grouped)
    core = lax.axis_index("seq")
    rows = attn_own.shape[0]
    depth = pieces[0].shape[0]
    half = pieces[0].shape[1]
    copies = []
    for i in range(count):
        for j in range(2):
            where = x if j == 0 else 1 - x
            start = where * depth if isinstance(x, int) else pl.multiple_of(where * depth, 32)
            copies.append(
                pltpu.make_async_copy(
                    pieces[2 * i + j], weights.at[i, pl.ds(start, depth)], sems.at[2 * i + j]
                )
            )
    start_all(copies)
    columns = pl.ds(pl.multiple_of(core * half, 128), half)
    cot_rows = jnp.concatenate([cot[:, columns], cot_far[...]], 0)
    total_now = total_in[...] if total_in is not None else None
    for i, number in enumerate(numbers):
        copies[2 * i].wait()
        copies[2 * i + 1].wait()
        back = dot(cot_rows, weights[i], COLS)
        near[:, i * 2 * depth : (i + 1) * 2 * depth] = back[:rows]
        far[:, i * 2 * depth : (i + 1) * 2 * depth] = back[rows:]
        place = pl.ds(pl.multiple_of(places[number] * 2 * depth, 128), 2 * depth)
        attn_rows = jnp.concatenate([attn_own[:, place], attn_far[:, place]], 0)
        term = dot(attn_rows, weights[i])
        total_now = term if total_now is None else total_now + term
    if last:
        own[...] = total_now[:rows]
        away[...] = total_now[rows:].astype(BF16)
    else:
        total[...] = total_now


def backward_kernel(grouped, numbers, *refs):
    (q, ko, kf, kt, vo, vf, vt, attn, near, far, act_grad, down) = refs[:12]
    dq, own, away, qs, keys, values, attns, downs, sems = refs[12:]
    count = len(numbers)
    rows = q.shape[0]
    width = qs.shape[2]
    places, _ = batch_places(grouped)
    copies = []
    for i, number in enumerate(numbers):
        place = pl.ds(pl.multiple_of(places[number] * width, 128), width)
        moves = [(q.at[:, place], qs.at[i]), (attn.at[:, place], attns.at[i])]
        moves.append((down.at[place], downs.at[i]))
        for j, (k, v) in enumerate(((ko, vo), (kf, vf), (kt, vt))):
            moves.append((k.at[:, place], keys.at[i, pl.ds(j * rows, rows)]))
            moves.append((v.at[:, place], values.at[i, pl.ds(j * rows, rows)]))
        group = [
            pltpu.make_async_copy(source, target, sems.at[i, j])
            for j, (source, target) in enumerate(moves)
        ]
        start_all(group)
        copies.append(group)
    for i in range(count):
        for copy in copies[i]:
            copy.wait()
        span = slice(i * width, (i + 1) * width)
        grad = (near[:, span] + far[:, span] + dot(act_grad[...], downs[i], COLS)).astype(BF16)
        for h in range(width // HD):
            c = slice(h * HD, (h + 1) * HD)
            o = slice(i * width + h * HD, i * width + (h + 1) * HD)
            prob = softmax_parts(qs[i, :, c], keys[i, :, c])
            prob_half = prob.astype(BF16)
            head = grad[:, c]
            delta = jnp.sum(head.astype(F32) * attns[i, :, c].astype(F32), -1, keepdims=True)
            prob_grad = dot(head, values[i, :, c], COLS)
            score_grad = (prob * (prob_grad - delta)).astype(BF16)
            dq[:, o] = (dot(score_grad, keys[i, :, c]) * FACTOR).astype(BF16)
            key_term = dot(score_grad[:, : 2 * rows], qs[i, :, c], ROWS)
            value_term = dot(prob_half[:, : 2 * rows], head, ROWS)
            own[0, :, o] = key_term[:rows]
            own[1, :, o] = value_term[:rows]
            away[0, :, o] = key_term[rows:].astype(BF16)
            away[1, :, o] = value_term[rows:].astype(BF16)


def finish_kernel(grouped, groups, *refs):
    count = len(groups)
    dq_parts, owns, aways = refs[:count], refs[count : 2 * count], refs[2 * count : 3 * count]
    own, away, act, up, update, dq, dk, dv = refs[3 * count :]
    places, _ = batch_places(grouped)
    core = lax.axis_index("seq")
    half = own.shape[1]
    for c, term in ((core, own[...]), (1 - core, away[...].astype(F32))):
        columns = pl.ds(pl.multiple_of(c * half, 128), half)
        update[:, columns] = (term + dot(act[...], up[:, columns])).astype(BF16)
    width = dq.shape[1] // BATCHES
    for g, numbers in enumerate(groups):
        for i, number in enumerate(numbers):
            place = pl.ds(pl.multiple_of(places[number] * width, 128), width)
            o = slice(i * width, (i + 1) * width)
            dq[:, place] = dq_parts[g][:, o]
            for j, target in enumerate((dk, dv)):
                value = owns[g][j, :, o] + aways[g][j, :, o].astype(F32)
                target[:, place] = (value * FACTOR if j == 0 else value).astype(BF16)


VMEM = pl.BlockSpec(memory_space=pltpu.VMEM)
ANY = pl.BlockSpec(memory_space=pl.ANY)


def shape(dims, dtype=BF16):
    return jax.ShapeDtypeStruct(dims, dtype)


def call(kernel, args, outs, in_specs, scratch, flops, megabytes):
    moved = sum(a.size * a.dtype.itemsize for a in (*args, *outs))
    return pl.pallas_call(
        kernel,
        out_shape=outs,
        in_specs=in_specs,
        out_specs=[VMEM] * len(outs),
        scratch_shapes=scratch,
        compiler_params=pltpu.CompilerParams(vmem_limit_bytes=megabytes * 2**20),
        cost_estimate=pl.CostEstimate(flops=flops, bytes_accessed=moved, transcendentals=0),
    )(*args)


def local(
    queries,
    image_keys,
    image_values,
    text_keys,
    text_values,
    control_hint,
    proj_out,
    adapter_down,
    adapter_up,
    cotangent,
):
    shards = lax.axis_size("fsdp")
    grouped = shards == 8 and lax.axis_size("rep") == 2 and lax.axis_size("seq") == 2
    q, ko, vo = queries[0], image_keys[0], image_values[0]
    kt, vt, hint, cot = text_keys[0], text_values[0], control_hint[0], cotangent[0]
    rows, inner = q.shape
    wide = cot.shape[1]
    half = proj_out.shape[1]
    rank = hint.shape[1]
    depth = inner // (2 * BATCHES)
    width = 2 * depth
    core = lax.axis_index("seq")
    scale = float(shards * lax.axis_size("seq") * rows) ** (-0.5)

    if grouped:
        z1 = ring_step(proj_out)
        x1 = swap(proj_out, "fsdp", 1)
        down_half = lax.dynamic_slice_in_dim(adapter_down, core * 96, 96, 0)
        up_half = lax.dynamic_slice_in_dim(adapter_up, core * 64, 64, 0)
        block = jnp.concatenate([down_half] + [up_half[:, 128 * j : 128 * j + 128] for j in range(3)], 0)[None]
        block = jnp.concatenate([block, swap(block, "fsdp", 2)], 0)
        both = swap(block, "fsdp", 4)
        block = jnp.concatenate([block, both], 0)
        mine = jnp.concatenate([block, swap(block, "fsdp", 1)], 0)
        theirs = swap(mine, "seq", 1)
        kf, vf = swap(ko, "seq", 1), swap(vo, "seq", 1)
        z2 = ring_step(z1)
        x2 = swap(z1, "fsdp", 1)
        y1 = swap(z1, "rep", 1)
        x3 = swap(z2, "fsdp", 1)
        y2 = swap(x2, "rep", 1)
        pieces = [proj_out, x1, z1, x2, y1, y2, z2, x3]
        adapters = (mine, theirs)
    else:
        half_out = lax.all_gather(proj_out, "fsdp", axis=0, tiled=True)
        pieces = [half_out[i * depth : (i + 1) * depth] for i in range(2 * BATCHES)]
        adapters = (
            lax.all_gather(adapter_down, "fsdp", axis=0, tiled=True),
            lax.all_gather(adapter_up, "fsdp", axis=1, tiled=True),
        )
        kf, vf = swap(ko, "seq", 1), swap(vo, "seq", 1)
    cot_far = swap(lax.dynamic_slice_in_dim(cot, (1 - core) * half, half, 1), "seq", 1)

    attention_flops = 2 * rows * 3 * rows * inner
    (attn,) = call(
        forward_kernel,
        (q, ko, kf, kt, vo, vf, vt),
        [shape((rows, inner))],
        [VMEM] + [ANY] * 6,
        [
            pltpu.VMEM((3 * rows, inner), BF16),
            pltpu.VMEM((3 * rows, inner), BF16),
            pltpu.SemaphoreType.DMA((2, 3)),
        ],
        40 * attention_flops,
        16,
    )
    attn_far = swap(attn, "seq", 1)
    outs = [
        shape((inner, rank)),
        shape((rank, wide)),
        shape((rows, rank)),
        shape((rows, rank)),
    ]
    if grouped:
        outs += [shape((8, 288, rank), F32)] * 2
        scratch = [pltpu.VMEM((inner + wide, rank), F32), pltpu.SemaphoreType.DMA((64,))]
    else:
        outs += [shape((inner, rank), F32), shape((wide, rank), F32)]
        scratch = [pltpu.SemaphoreType.DMA((2,))]
    down, up, act, act_grad, first_term, second_term = call(
        functools.partial(adapter_kernel, grouped, scale),
        (*adapters, attn, cot, hint),
        outs,
        [ANY, ANY, VMEM, VMEM, VMEM],
        scratch,
        40 * rows * (inner + wide) * rank,
        24,
    )
    if grouped:
        term = first_term + swap(second_term, "seq", 1)
        for mask in (1, 4, 2):
            keep = term.shape[0] // 2
            term = term[:keep] + swap(term[keep:].astype(BF16), "fsdp", mask).astype(F32)
        down_grad, up_grad = term[0, :96], term[0, 96:].T
    else:
        down_grad = lax.psum_scatter(first_term, ("fsdp", "seq"), scatter_dimension=0, tiled=True)
        up_grad = lax.psum_scatter(second_term, ("fsdp", "seq"), scatter_dimension=0, tiled=True).T

    groups = ((0, 1), (2, 3))
    total = None
    dqs, owns, aways = [], [], []
    for numbers in groups:
        count = len(numbers)
        last = numbers[-1] == BATCHES - 1
        args = [pieces[2 * n + j] for n in numbers for j in range(2)] + [attn, attn_far, cot, cot_far]
        if total is not None:
            args.append(total)
        outs = [shape((rows, count * width), F32)] * 2
        if last:
            outs += [shape((rows, half), F32), shape((rows, half))]
        else:
            outs += [shape((2 * rows, half), F32)]
        results = call(
            functools.partial(project_kernel, grouped, numbers, last),
            tuple(args),
            outs,
            [ANY] * (2 * count) + [VMEM] * (len(args) - 2 * count),
            [pltpu.VMEM((count, width, half), BF16), pltpu.SemaphoreType.DMA((2 * count,))],
            8 * 2 * rows * count * width * half * 2,
            24,
        )
        near, far = results[:2]
        if last:
            own_update, away_update = results[2], swap(results[3], "seq", 1)
        else:
            total = results[2]
        dq, own, away = call(
            functools.partial(backward_kernel, grouped, numbers),
            (q, ko, kf, kt, vo, vf, vt, attn, near, swap(far, "seq", 1), act_grad, down),
            [
                shape((rows, count * width)),
                shape((2, rows, count * width), F32),
                shape((2, rows, count * width)),
            ],
            [ANY] * 8 + [VMEM] * 3 + [ANY],
            [
                pltpu.VMEM((count, rows, width), BF16),
                pltpu.VMEM((count, 3 * rows, width), BF16),
                pltpu.VMEM((count, 3 * rows, width), BF16),
                pltpu.VMEM((count, rows, width), BF16),
                pltpu.VMEM((count, width, rank), BF16),
                pltpu.SemaphoreType.DMA((count, 9)),
            ],
            60 * attention_flops,
            16,
        )
        dqs.append(dq)
        owns.append(own)
        aways.append(swap(away, "seq", 1))
    update, query_grad, key_grad, value_grad = call(
        functools.partial(finish_kernel, grouped, groups),
        (*dqs, *owns, *aways, own_update, away_update, act, up),
        [shape((rows, wide))] + [shape((rows, inner))] * 3,
        [VMEM] * (3 * len(groups) + 4),
        [],
        2 * rows * rank * wide,
        24,
    )
    return (update[None], query_grad[None], key_grad[None], value_grad[None], down_grad, up_grad)


def solution(mesh):
    rows = P(("rep", "fsdp"), "seq", None)
    text = P(("rep", "fsdp"), None, None)
    return jax.shard_map(
        local,
        mesh=mesh,
        in_specs=(
            rows,
            rows,
            rows,
            text,
            text,
            rows,
            P("fsdp", "seq"),
            P("fsdp", None),
            P(None, "fsdp"),
            rows,
        ),
        out_specs=(rows, rows, rows, rows, P(("rep", "fsdp", "seq"), None), P("rep", ("fsdp", "seq"))),
        check_vma=False,
    )
```

```python
import functools

import jax
import jax.numpy as jnp
from jax import lax
from jax.experimental import pallas as pl
from jax.experimental.pallas import tpu as pltpu
from jax.sharding import PartitionSpec as P

HD = 128
BATCHES = 4
FACTOR = HD ** (-0.5)
F32 = jnp.float32
BF16 = jnp.bfloat16
ROWS = (((0,), (0,)), ((), ()))
COLS = (((1,), (1,)), ((), ()))


def swap(value, axis, mask):
    pairs = [(source, source ^ mask) for source in range(lax.axis_size(axis))]
    return lax.ppermute(value, axis, pairs)


def ring_after(z):
    low, high = z % 2, z // 2
    return 2 * low + (1 - high)


def ring_before(z):
    low, high = z % 2, z // 2
    return 2 * (1 - low) + high


def ring_step(value, back=False, turn=0):
    pairs = []
    for f in range(8):
        z, x = f // 2, (f % 2) ^ turn
        pairs.append((f, ring_after(z) * 2 + x))
        pairs.append((8 + f, 8 + ring_before(z) * 2 + x))
    if back:
        pairs = [(target, source) for source, target in pairs]
    return lax.ppermute(value, ("rep", "fsdp"), pairs)


def dot(a, b, dims=None):
    if dims is None:
        return jnp.dot(a, b, preferred_element_type=F32)
    return lax.dot_general(a, b, dims, preferred_element_type=F32)


def batch_places(grouped):
    if not grouped:
        return list(range(BATCHES)), 0
    f = lax.axis_index("fsdp")
    rep = lax.axis_index("rep")
    z, x = f // 2, f % 2
    after, before = ring_after(z), ring_before(z)
    first = jnp.where(rep == 0, before, after)
    second = jnp.where(rep == 0, after, before)
    return [z, first, second, 3 - z], x


def softmax_parts(q, k):
    scores = dot(q, k, COLS) * FACTOR
    top = jnp.max(scores, -1, keepdims=True)
    weight = jnp.exp(scores - top)
    return weight * (1.0 / jnp.sum(weight, -1, keepdims=True))


def start_all(copies):
    for copy in copies:
        copy.start()


def forward_kernel(q_in, ko, kf, kt, vo, vf, vt, attn, q, keys, values, sems):
    rows, inner = q.shape
    copies = [pltpu.make_async_copy(q_in, q, sems.at[2, 0])]
    copies += [
        pltpu.make_async_copy(source, target.at[pl.ds(i * rows, rows)], sems.at[j, i])
        for j, (sources, target) in enumerate((((ko, kf, kt), keys), ((vo, vf, vt), values)))
        for i, source in enumerate(sources)
    ]
    start_all(copies)
    for copy in copies:
        copy.wait()
    for h in range(inner // HD):
        c = slice(h * HD, (h + 1) * HD)
        prob = softmax_parts(q[:, c], keys[:, c]).astype(BF16)
        attn[:, c] = dot(prob, values[:, c]).astype(BF16)


def pack_kernel(proj, down_in, up_in, message, down, up, sems):
    depth = proj.shape[0]
    copies = [
        pltpu.make_async_copy(down_in, down, sems.at[0]),
        pltpu.make_async_copy(up_in, up, sems.at[1]),
        pltpu.make_async_copy(proj, message.at[pl.ds(0, depth)], sems.at[2]),
    ]
    start_all(copies)
    copies[0].wait()
    copies[1].wait()
    for j in range(12):
        c = slice(128 * j, 128 * j + 128)
        message[depth : depth + 16, c] = down[16 * j : 16 * j + 16]
        a, b = j // 3, j % 3
        message[depth + 16 : depth + 48, c] = up[32 * a : 32 * a + 32, 128 * b : 128 * b + 128]
    copies[2].wait()


def adapter_kernel(packed, scale, *refs):
    if packed:
        sources, refs = refs[:8], refs[8:]
        (attn, cot, hint, down, up, act, act_grad, near, far, terms, messages, sems) = refs
        f = lax.axis_index("fsdp")
        core = lax.axis_index("seq")
        places, x = batch_places(True)
        copies = []
        for i, source in enumerate(sources):
            behind = source.shape[0] - 48
            copies.append(pltpu.make_async_copy(source.at[pl.ds(behind, 48)], messages.at[i], sems.at[i]))
        start_all(copies)
        for i, copy in enumerate(copies):
            copy.wait()
            block = places[i // 2] * 2 + (x if i % 2 == 0 else 1 - x)
            for j in range(12):
                c = slice(128 * j, 128 * j + 128)
                down[pl.ds(pl.multiple_of(block * 192 + 16 * j, 16), 16)] = messages[i, 0:16, c]
                a, b = j // 3, j % 3
                columns = pl.ds(pl.multiple_of(block * 384 + 128 * b, 128), 128)
                up[32 * a : 32 * a + 32, columns] = messages[i, 16:48, c]
    else:
        (down_in, up_in, attn, cot, hint, down, up, act, act_grad, down_term, up_term, sems) = refs
        copies = [
            pltpu.make_async_copy(down_in, down, sems.at[0]),
            pltpu.make_async_copy(up_in, up, sems.at[1]),
        ]
        start_all(copies)
        for copy in copies:
            copy.wait()
    pre_act = dot(attn[...], down[...]) + hint[...].astype(F32)
    logistic = 1.0 / (1.0 + jnp.exp(-pre_act))
    act[...] = (pre_act * logistic).astype(BF16)
    act_back = dot(cot[...], up[...], COLS)
    act_grad[...] = (act_back * logistic * (1.0 + pre_act * (1.0 - logistic))).astype(BF16)
    inner, wide = attn.shape[1], cot.shape[1]
    if not packed:
        down_term[...] = dot(attn[...], act_grad[...], ROWS) * scale
        up_term[...] = dot(cot[...], act[...], ROWS) * scale
        return
    terms[pl.ds(0, inner)] = dot(attn[...], act_grad[...], ROWS) * scale
    terms[pl.ds(inner, wide)] = dot(cot[...], act[...], ROWS) * scale
    for place in range(8):
        block = f ^ place
        for target, half in ((near, core), (far, 1 - core)):
            piece = block * 2 + half
            rows = terms[pl.ds(pl.multiple_of(piece * 96, 32), 96)]
            target[place, 0:96] = rows.astype(target.dtype)
            rows = terms[pl.ds(pl.multiple_of(inner + piece * 192, 64), 192)]
            target[place, 96:288] = rows.astype(target.dtype)


def project_kernel(grouped, numbers, *refs):
    count = len(numbers)
    pieces = refs[: 2 * count]
    attn_own, attn_far, cot, cot_far = refs[2 * count : 2 * count + 4]
    rest = refs[2 * count + 4 :]
    carried = ()
    if numbers == (1,):
        carried, rest = rest[:2], rest[2:]
    total_in = None
    if numbers[0] > 0:
        total_in, rest = rest[0], rest[1:]
    last = numbers[-1] == BATCHES - 1
    if last:
        near, far, own, away, weights, sems = rest
    else:
        near, far, total, weights, sems = rest
    places, x = batch_places(grouped)
    core = lax.axis_index("seq")
    rows = attn_own.shape[0]
    depth = attn_own.shape[1] // (2 * BATCHES)
    half = pieces[0].shape[1]
    copies = []
    for i in range(count):
        for j in range(2):
            where = (x if j == 0 else 1 - x) * depth
            copies.append(
                pltpu.make_async_copy(
                    pieces[2 * i + j].at[pl.ds(0, depth)],
                    weights.at[i, pl.ds(where if isinstance(x, int) else pl.multiple_of(where, 32), depth)],
                    sems.at[2 * i + j],
                )
            )
    start_all(copies)
    columns = pl.ds(pl.multiple_of(core * half, 128), half)
    cot_rows = jnp.concatenate([cot[:, columns], cot_far[...]], 0)
    total_now = total_in[...] if total_in is not None else None
    base = 0
    if carried:
        base = carried[0].shape[1]
        near[:, :base] = carried[0][...]
        far[:, :base] = carried[1][...]
    for i, number in enumerate(numbers):
        for copy in copies[2 * i : 2 * i + 2]:
            copy.wait()
        back = dot(cot_rows, weights[i], COLS)
        span = slice(base + i * 2 * depth, base + (i + 1) * 2 * depth)
        near[:, span] = back[:rows]
        far[:, span] = back[rows:].astype(BF16)
        place = pl.ds(pl.multiple_of(places[number] * 2 * depth, 128), 2 * depth)
        attn_rows = jnp.concatenate([attn_own[:, place], attn_far[:, place]], 0)
        term = dot(attn_rows, weights[i])
        total_now = term if total_now is None else total_now + term
    if last:
        own[...] = total_now[:rows]
        away[...] = total_now[rows:].astype(BF16)
    else:
        total[...] = total_now


def backward_kernel(grouped, numbers, *refs):
    (q, ko, kf, kt, vo, vf, vt, attn, near, far, act_grad, down) = refs[:12]
    dq, own, away, qs, keys, values, attns, downs, sems = refs[12:]
    count = len(numbers)
    rows = q.shape[0]
    width = qs.shape[2]
    places, _ = batch_places(grouped)
    copies = []
    for i, number in enumerate(numbers):
        place = pl.ds(pl.multiple_of(places[number] * width, 128), width)
        moves = [(q.at[:, place], qs.at[i]), (attn.at[:, place], attns.at[i])]
        moves.append((down.at[place], downs.at[i]))
        for j, (k, v) in enumerate(((ko, vo), (kf, vf), (kt, vt))):
            moves.append((k.at[:, place], keys.at[i, pl.ds(j * rows, rows)]))
            moves.append((v.at[:, place], values.at[i, pl.ds(j * rows, rows)]))
        group = [
            pltpu.make_async_copy(source, target, sems.at[i, j])
            for j, (source, target) in enumerate(moves)
        ]
        start_all(group)
        copies.append(group)
    for i in range(count):
        for copy in copies[i]:
            copy.wait()
        span = slice(i * width, (i + 1) * width)
        grad = (near[:, span] + far[:, span].astype(F32) + dot(act_grad[...], downs[i], COLS)).astype(BF16)
        for h in range(width // HD):
            c = slice(h * HD, (h + 1) * HD)
            o = slice(i * width + h * HD, i * width + (h + 1) * HD)
            prob = softmax_parts(qs[i, :, c], keys[i, :, c])
            prob_half = prob.astype(BF16)
            head = grad[:, c]
            delta = jnp.sum(head.astype(F32) * attns[i, :, c].astype(F32), -1, keepdims=True)
            prob_grad = dot(head, values[i, :, c], COLS)
            score_grad = (prob * (prob_grad - delta)).astype(BF16)
            dq[:, o] = (dot(score_grad, keys[i, :, c]) * FACTOR).astype(BF16)
            key_term = dot(score_grad[:, : 2 * rows], qs[i, :, c], ROWS)
            value_term = dot(prob_half[:, : 2 * rows], head, ROWS)
            own[0, :, o] = key_term[:rows]
            own[1, :, o] = value_term[:rows]
            away[0, :, o] = key_term[rows:].astype(BF16)
            away[1, :, o] = value_term[rows:].astype(BF16)


def update_kernel(own, away, act, up, *refs):
    if len(refs) == 1:
        (update,) = refs
    else:
        term, term_far, update, down_grad, up_grad = refs
        value = term[0] + term_far[...].astype(F32)
        rows = down_grad.shape[0]
        down_grad[...] = value[:rows]
        up_grad[...] = value[rows:].T
    core = lax.axis_index("seq")
    half = own.shape[1]
    for c, term in ((core, own[...]), (1 - core, away[...].astype(F32))):
        columns = pl.ds(pl.multiple_of(c * half, 128), half)
        update[:, columns] = (term + dot(act[...], up[:, columns])).astype(BF16)


def finish_kernel(grouped, groups, *refs):
    count = len(groups)
    dq_parts, owns, aways = refs[:count], refs[count : 2 * count], refs[2 * count : 3 * count]
    dq, dk, dv = refs[3 * count :]
    places, _ = batch_places(grouped)
    width = dq.shape[1] // BATCHES
    for g, numbers in enumerate(groups):
        for i, number in enumerate(numbers):
            place = pl.ds(pl.multiple_of(places[number] * width, 128), width)
            o = slice(i * width, (i + 1) * width)
            dq[:, place] = dq_parts[g][:, o]
            for j, target in enumerate((dk, dv)):
                value = owns[g][j, :, o] + aways[g][j, :, o].astype(F32)
                target[:, place] = (value * FACTOR if j == 0 else value).astype(BF16)


VMEM = pl.BlockSpec(memory_space=pltpu.VMEM)
ANY = pl.BlockSpec(memory_space=pl.ANY)
HBM = pl.BlockSpec(memory_space=pltpu.HBM)


def shape(dims, dtype=BF16):
    return jax.ShapeDtypeStruct(dims, dtype)


def call(kernel, args, outs, in_specs, scratch, flops, megabytes):
    return pl.pallas_call(
        kernel,
        out_shape=outs,
        in_specs=in_specs,
        out_specs=[VMEM] * len(outs),
        scratch_shapes=scratch,
        compiler_params=pltpu.CompilerParams(vmem_limit_bytes=megabytes * 2**20),
        cost_estimate=pl.CostEstimate(flops=int(flops), bytes_accessed=int(flops) // 400, transcendentals=0),
    )(*args)


def local(
    queries,
    image_keys,
    image_values,
    text_keys,
    text_values,
    control_hint,
    proj_out,
    adapter_down,
    adapter_up,
    cotangent,
):
    shards = lax.axis_size("fsdp")
    grouped = shards == 8 and lax.axis_size("rep") == 2 and lax.axis_size("seq") == 2
    q, ko, vo = queries[0], image_keys[0], image_values[0]
    kt, vt, hint, cot = text_keys[0], text_values[0], control_hint[0], cotangent[0]
    rows, inner = q.shape
    wide = cot.shape[1]
    half = proj_out.shape[1]
    rank = hint.shape[1]
    depth = inner // (2 * BATCHES)
    width = 2 * depth
    core = lax.axis_index("seq")
    scale = float(shards * lax.axis_size("seq") * rows) ** (-0.5)

    kf, vf = swap(ko, "seq", 1), swap(vo, "seq", 1)
    cot_far = swap(lax.dynamic_slice_in_dim(cot, (1 - core) * half, half, 1), "seq", 1)
    attention_flops = 2 * rows * 3 * rows * inner
    (attn,) = call(
        forward_kernel,
        (q, ko, kf, kt, vo, vf, vt),
        [shape((rows, inner))],
        [HBM, HBM, ANY, HBM, HBM, ANY, HBM],
        [
            pltpu.VMEM((rows, inner), BF16),
            pltpu.VMEM((3 * rows, inner), BF16),
            pltpu.VMEM((3 * rows, inner), BF16),
            pltpu.SemaphoreType.DMA((3, 3)),
        ],
        attention_flops,
        16,
    )
    if grouped:
        (message,) = call(
            pack_kernel,
            (proj_out, adapter_down, adapter_up),
            [shape((depth + 48, half))],
            [HBM] * 3,
            [
                pltpu.VMEM(adapter_down.shape, BF16),
                pltpu.VMEM(adapter_up.shape, BF16),
                pltpu.SemaphoreType.DMA((3,)),
            ],
            1000,
            16,
        )
        z1, x1 = ring_step(message), swap(message, "fsdp", 1)
        z1, x1, attn, cot_far = lax.optimization_barrier((z1, x1, attn, cot_far))
        z2, x2, y1 = ring_step(z1), swap(z1, "fsdp", 1), swap(z1, "rep", 1)
        end_x, end_y = ring_step(z1[depth:], turn=1), ring_step(x1[depth:], back=True)
    else:
        half_out = lax.all_gather(proj_out, "fsdp", axis=0, tiled=True)
        pieces = [half_out[i * depth : (i + 1) * depth] for i in range(2 * BATCHES)]
        adapters = (
            lax.all_gather(adapter_down, "fsdp", axis=0, tiled=True),
            lax.all_gather(adapter_up, "fsdp", axis=1, tiled=True),
        )
    attn_far = swap(attn, "seq", 1)

    def project(numbers, pieces, *carried):
        count = len(numbers)
        done = sum(numbers) if numbers == (1,) else 0
        outs = [shape((rows, (count + done) * width), F32), shape((rows, (count + done) * width))]
        if numbers[-1] == BATCHES - 1:
            outs += [shape((rows, half), F32), shape((rows, half))]
        else:
            outs += [shape((2 * rows, half), F32)]
        args = (*pieces, attn, attn_far, cot, cot_far, *carried)
        return call(
            functools.partial(project_kernel, grouped, numbers),
            args,
            outs,
            [ANY] * (2 * count) + [VMEM] * (len(args) - 2 * count),
            [pltpu.VMEM((count, width, half), BF16), pltpu.SemaphoreType.DMA((2 * count,))],
            (8 if numbers[-1] > 1 else 0.1) * 2 * rows * count * width * half * 2,
            24,
        )

    near, far, total = project((0,), [message, x1] if grouped else pieces[:2])
    if grouped:
        z2, x2, y1, end_x, end_y, total = lax.optimization_barrier((z2, x2, y1, end_x, end_y, total))
        x3, y2 = swap(z2[:depth], "fsdp", 1), swap(x2[:depth], "rep", 1)
        pieces = [message, x1, z1, x2, y1, y2, z2, x3]
        adapters = (message, x1, z1, x2, y1, end_y, z2, end_x)
    outs = [
        shape((inner, rank)),
        shape((rank, wide)),
        shape((rows, rank)),
        shape((rows, rank)),
    ]
    if grouped:
        outs += [shape((8, 288, rank), F32), shape((8, 288, rank))]
        scratch = [
            pltpu.VMEM((inner + wide, rank), F32),
            pltpu.VMEM((8, 48, half), BF16),
            pltpu.SemaphoreType.DMA((8,)),
        ]
    else:
        outs += [shape((inner, rank), F32), shape((wide, rank), F32)]
        scratch = [pltpu.SemaphoreType.DMA((2,))]
    down, up, act, act_grad, first_term, second_term = call(
        functools.partial(adapter_kernel, grouped, scale),
        (*adapters, attn, cot, hint),
        outs,
        [ANY] * len(adapters) + [VMEM] * 3,
        scratch,
        rows * (inner + wide) * rank,
        24,
    )
    def backward(numbers, near, far):
        count = len(numbers)
        return call(
            functools.partial(backward_kernel, grouped, numbers),
            (q, ko, kf, kt, vo, vf, vt, attn, near, far, act_grad, down),
            [
                shape((rows, count * width)),
                shape((2, rows, count * width), F32),
                shape((2, rows, count * width)),
            ],
            [HBM, HBM, ANY, HBM, HBM, ANY, HBM, ANY] + [VMEM] * 3 + [ANY],
            [
                pltpu.VMEM((count, rows, width), BF16),
                pltpu.VMEM((count, 3 * rows, width), BF16),
                pltpu.VMEM((count, 3 * rows, width), BF16),
                pltpu.VMEM((count, rows, width), BF16),
                pltpu.VMEM((count, width, rank), BF16),
                pltpu.SemaphoreType.DMA((count, 9)),
            ],
            (30 if numbers[-1] > 1 else 0.1) * attention_flops,
            16,
        )

    groups = ((0, 1), (2,), (3,))
    near, far, total = project((1,), pieces[2:4], near, far, total)
    far = swap(far, "seq", 1)
    if grouped:
        term = first_term + swap(second_term, "seq", 1).astype(F32)
        shares = [swap(term[2 * k : 2 * k + 2].astype(BF16), "fsdp", 2 * k) for k in (1, 2, 3)]
        term = term[:2] + (shares[0].astype(F32) + shares[1].astype(F32) + shares[2].astype(F32))
        term_far = swap(term[1].astype(BF16), "fsdp", 1)
    dq_a, own_a, away_a = backward(groups[0], near, far)
    away_a = swap(away_a, "seq", 1)
    if grouped:
        pieces[5], pieces[7], dq_a = lax.optimization_barrier((pieces[5], pieces[7], dq_a))
    near_b, far_b, total = project((2,), pieces[4:6], total)
    far_b = swap(far_b, "seq", 1)
    near_c, far_c, own_update, away_update = project((3,), pieces[6:8], total)
    far_c = swap(far_c, "seq", 1)
    away_update = swap(away_update, "seq", 1)
    dq_b, own_b, away_b = backward(groups[1], near_b, far_b)
    away_b = swap(away_b, "seq", 1)
    near_c, dq_b = lax.optimization_barrier((near_c, dq_b))
    dq_c, own_c, away_c = backward(groups[2], near_c, far_c)
    away_c = swap(away_c, "seq", 1)
    if not grouped:
        down_grad = lax.psum_scatter(first_term, ("fsdp", "seq"), scatter_dimension=0, tiled=True)
        up_grad = lax.psum_scatter(second_term, ("fsdp", "seq"), scatter_dimension=0, tiled=True).T
    args = [own_update, away_update, act, up]
    outs = [shape((rows, wide))]
    if grouped:
        args += [term, term_far]
        outs += [shape((96, rank), F32), shape((rank, 192), F32)]
    update, *adapter_grads = call(
        update_kernel, tuple(args), outs, [VMEM] * len(args), [], 2 * rows * rank * wide, 24
    )
    if grouped:
        down_grad, up_grad = adapter_grads
    args = (dq_a, dq_b, dq_c, own_a, own_b, own_c, away_a, away_b, away_c)
    query_grad, key_grad, value_grad = call(
        functools.partial(finish_kernel, grouped, groups),
        args,
        [shape((rows, inner))] * 3,
        [VMEM] * len(args),
        [],
        2 * rows * rank * wide,
        24,
    )
    return (update[None], query_grad[None], key_grad[None], value_grad[None], down_grad, up_grad)


def solution(mesh):
    rows = P(("rep", "fsdp"), "seq", None)
    text = P(("rep", "fsdp"), None, None)
    return jax.shard_map(
        local,
        mesh=mesh,
        in_specs=(
            rows,
            rows,
            rows,
            text,
            text,
            rows,
            P("fsdp", "seq"),
            P("fsdp", None),
            P(None, "fsdp"),
            rows,
        ),
        out_specs=(rows, rows, rows, rows, P(("rep", "fsdp", "seq"), None), P("rep", ("fsdp", "seq"))),
        check_vma=False,
    )
```

```python
import functools

import jax
import jax.numpy as jnp
from jax import lax
from jax.experimental import pallas as pl
from jax.experimental.pallas import tpu as pltpu
from jax.sharding import PartitionSpec as P

HD = 128
BATCHES = 4
FACTOR = HD ** (-0.5)
F32 = jnp.float32
BF16 = jnp.bfloat16
ROWS = (((0,), (0,)), ((), ()))
COLS = (((1,), (1,)), ((), ()))


def swap(value, axis, mask):
    pairs = [(source, source ^ mask) for source in range(lax.axis_size(axis))]
    return lax.ppermute(value, axis, pairs)


def ring_after(z):
    low, high = z % 2, z // 2
    return 2 * low + (1 - high)


def ring_before(z):
    low, high = z % 2, z // 2
    return 2 * (1 - low) + high


def ring_step(value, back=False, turn=0):
    pairs = []
    for f in range(8):
        z, x = f // 2, (f % 2) ^ turn
        pairs.append((f, ring_after(z) * 2 + x))
        pairs.append((8 + f, 8 + ring_before(z) * 2 + x))
    if back:
        pairs = [(target, source) for source, target in pairs]
    return lax.ppermute(value, ("rep", "fsdp"), pairs)


def dot(a, b, dims=None):
    if dims is None:
        return jnp.dot(a, b, preferred_element_type=F32)
    return lax.dot_general(a, b, dims, preferred_element_type=F32)


def batch_places(grouped):
    if not grouped:
        return list(range(BATCHES)), 0
    f = lax.axis_index("fsdp")
    rep = lax.axis_index("rep")
    z, x = f // 2, f % 2
    after, before = ring_after(z), ring_before(z)
    first = jnp.where(rep == 0, before, after)
    second = jnp.where(rep == 0, after, before)
    return [z, first, second, 3 - z], x


def softmax_parts(q, k):
    scores = dot(q, k, COLS) * FACTOR
    top = jnp.max(scores, -1, keepdims=True)
    weight = jnp.exp(scores - top)
    return weight * (1.0 / jnp.sum(weight, -1, keepdims=True))


def start_all(copies):
    for copy in copies:
        copy.start()


def forward_kernel(q_in, ko, kf, kt, vo, vf, vt, attn, q, keys, values, sems):
    rows, inner = q.shape
    copies = [pltpu.make_async_copy(q_in, q, sems.at[2, 0])]
    copies += [
        pltpu.make_async_copy(source, target.at[pl.ds(i * rows, rows)], sems.at[j, i])
        for j, (sources, target) in enumerate((((ko, kf, kt), keys), ((vo, vf, vt), values)))
        for i, source in enumerate(sources)
    ]
    start_all(copies)
    for copy in copies:
        copy.wait()
    for h in range(inner // HD):
        c = slice(h * HD, (h + 1) * HD)
        prob = softmax_parts(q[:, c], keys[:, c]).astype(BF16)
        attn[:, c] = dot(prob, values[:, c]).astype(BF16)


def pack_kernel(proj, down_in, up_in, message, down, up, sems):
    depth = proj.shape[0]
    copies = [
        pltpu.make_async_copy(down_in, down, sems.at[0]),
        pltpu.make_async_copy(up_in, up, sems.at[1]),
        pltpu.make_async_copy(proj, message.at[pl.ds(0, depth)], sems.at[2]),
    ]
    start_all(copies)
    copies[0].wait()
    copies[1].wait()
    for j in range(12):
        c = slice(128 * j, 128 * j + 128)
        message[depth : depth + 16, c] = down[16 * j : 16 * j + 16]
        a, b = j // 3, j % 3
        message[depth + 16 : depth + 48, c] = up[32 * a : 32 * a + 32, 128 * b : 128 * b + 128]
    copies[2].wait()


def adapter_kernel(packed, scale, *refs):
    if packed:
        sources, refs = refs[:8], refs[8:]
        (attn, cot, hint, down, up, act, act_grad, near, far, terms, messages, sems) = refs
        f = lax.axis_index("fsdp")
        core = lax.axis_index("seq")
        places, x = batch_places(True)
        copies = []
        for i, source in enumerate(sources):
            behind = source.shape[0] - 48
            copies.append(pltpu.make_async_copy(source.at[pl.ds(behind, 48)], messages.at[i], sems.at[i]))
        start_all(copies)
        for i, copy in enumerate(copies):
            copy.wait()
            block = places[i // 2] * 2 + (x if i % 2 == 0 else 1 - x)
            for j in range(12):
                c = slice(128 * j, 128 * j + 128)
                down[pl.ds(pl.multiple_of(block * 192 + 16 * j, 16), 16)] = messages[i, 0:16, c]
                a, b = j // 3, j % 3
                columns = pl.ds(pl.multiple_of(block * 384 + 128 * b, 128), 128)
                up[32 * a : 32 * a + 32, columns] = messages[i, 16:48, c]
    else:
        (down_in, up_in, attn, cot, hint, down, up, act, act_grad, down_term, up_term, sems) = refs
        copies = [
            pltpu.make_async_copy(down_in, down, sems.at[0]),
            pltpu.make_async_copy(up_in, up, sems.at[1]),
        ]
        start_all(copies)
        for copy in copies:
            copy.wait()
    pre_act = dot(attn[...], down[...]) + hint[...].astype(F32)
    logistic = 1.0 / (1.0 + jnp.exp(-pre_act))
    act[...] = (pre_act * logistic).astype(BF16)
    act_back = dot(cot[...], up[...], COLS)
    act_grad[...] = (act_back * logistic * (1.0 + pre_act * (1.0 - logistic))).astype(BF16)
    inner, wide = attn.shape[1], cot.shape[1]
    if not packed:
        down_term[...] = dot(attn[...], act_grad[...], ROWS) * scale
        up_term[...] = dot(cot[...], act[...], ROWS) * scale
        return
    terms[pl.ds(0, inner)] = dot(attn[...], act_grad[...], ROWS) * scale
    terms[pl.ds(inner, wide)] = dot(cot[...], act[...], ROWS) * scale
    for place, mask in enumerate((0, 1, 4, 5, 2, 3, 6, 7)):
        block = f ^ mask
        for target, half in ((near, core), (far, 1 - core)):
            piece = block * 2 + half
            rows = terms[pl.ds(pl.multiple_of(piece * 96, 32), 96)]
            target[place, 0:96] = rows.astype(target.dtype)
            rows = terms[pl.ds(pl.multiple_of(inner + piece * 192, 64), 192)]
            target[place, 96:288] = rows.astype(target.dtype)


def project_kernel(grouped, numbers, *refs):
    count = len(numbers)
    pieces = refs[: 2 * count]
    attn_own, attn_far, cot, cot_far = refs[2 * count : 2 * count + 4]
    rest = refs[2 * count + 4 :]
    carried = ()
    if numbers == (1,):
        carried, rest = rest[:2], rest[2:]
    total_in = None
    if numbers[0] > 0:
        total_in, rest = rest[0], rest[1:]
    last = numbers[-1] == BATCHES - 1
    if last:
        near, far, own, away, weights, sems = rest
    else:
        near, far, total, weights, sems = rest
    places, x = batch_places(grouped)
    core = lax.axis_index("seq")
    rows = attn_own.shape[0]
    depth = attn_own.shape[1] // (2 * BATCHES)
    half = pieces[0].shape[1]
    copies = []
    for i in range(count):
        for j in range(2):
            where = (x if j == 0 else 1 - x) * depth
            copies.append(
                pltpu.make_async_copy(
                    pieces[2 * i + j].at[pl.ds(0, depth)],
                    weights.at[i, pl.ds(where if isinstance(x, int) else pl.multiple_of(where, 32), depth)],
                    sems.at[2 * i + j],
                )
            )
    start_all(copies)
    columns = pl.ds(pl.multiple_of(core * half, 128), half)
    cot_rows = jnp.concatenate([cot[:, columns], cot_far[...]], 0)
    total_now = total_in[...] if total_in is not None else None
    base = 0
    if carried:
        base = carried[0].shape[1]
        near[:, :base] = carried[0][...]
        far[:, :base] = carried[1][...]
    for i, number in enumerate(numbers):
        for copy in copies[2 * i : 2 * i + 2]:
            copy.wait()
        back = dot(cot_rows, weights[i], COLS)
        span = slice(base + i * 2 * depth, base + (i + 1) * 2 * depth)
        near[:, span] = back[:rows]
        far[:, span] = back[rows:].astype(BF16)
        place = pl.ds(pl.multiple_of(places[number] * 2 * depth, 128), 2 * depth)
        attn_rows = jnp.concatenate([attn_own[:, place], attn_far[:, place]], 0)
        term = dot(attn_rows, weights[i])
        total_now = term if total_now is None else total_now + term
    if last:
        own[...] = total_now[:rows]
        away[...] = total_now[rows:].astype(BF16)
    else:
        total[...] = total_now


def backward_kernel(grouped, numbers, *refs):
    (q, ko, kf, kt, vo, vf, vt, attn, near, far, act_grad, down) = refs[:12]
    dq, own, away, qs, keys, values, attns, downs, sems = refs[12:]
    count = len(numbers)
    rows = q.shape[0]
    width = qs.shape[2]
    places, _ = batch_places(grouped)
    copies = []
    for i, number in enumerate(numbers):
        place = pl.ds(pl.multiple_of(places[number] * width, 128), width)
        moves = [(q.at[:, place], qs.at[i]), (attn.at[:, place], attns.at[i])]
        moves.append((down.at[place], downs.at[i]))
        for j, (k, v) in enumerate(((ko, vo), (kf, vf), (kt, vt))):
            moves.append((k.at[:, place], keys.at[i, pl.ds(j * rows, rows)]))
            moves.append((v.at[:, place], values.at[i, pl.ds(j * rows, rows)]))
        group = [
            pltpu.make_async_copy(source, target, sems.at[i, j])
            for j, (source, target) in enumerate(moves)
        ]
        start_all(group)
        copies.append(group)
    for i in range(count):
        for copy in copies[i]:
            copy.wait()
        span = slice(i * width, (i + 1) * width)
        grad = (near[:, span] + far[:, span].astype(F32) + dot(act_grad[...], downs[i], COLS)).astype(BF16)
        for h in range(width // HD):
            c = slice(h * HD, (h + 1) * HD)
            o = slice(i * width + h * HD, i * width + (h + 1) * HD)
            prob = softmax_parts(qs[i, :, c], keys[i, :, c])
            prob_half = prob.astype(BF16)
            head = grad[:, c]
            delta = jnp.sum(head.astype(F32) * attns[i, :, c].astype(F32), -1, keepdims=True)
            prob_grad = dot(head, values[i, :, c], COLS)
            score_grad = (prob * (prob_grad - delta)).astype(BF16)
            dq[:, o] = (dot(score_grad, keys[i, :, c]) * FACTOR).astype(BF16)
            key_term = dot(score_grad[:, : 2 * rows], qs[i, :, c], ROWS)
            value_term = dot(prob_half[:, : 2 * rows], head, ROWS)
            own[0, :, o] = key_term[:rows]
            own[1, :, o] = value_term[:rows]
            away[0, :, o] = key_term[rows:].astype(BF16)
            away[1, :, o] = value_term[rows:].astype(BF16)


def update_kernel(own, away, act, up, *refs):
    if len(refs) == 1:
        (update,) = refs
    else:
        term, term_far, update, down_grad, up_grad = refs
        value = term[0] + term_far[...].astype(F32)
        rows = down_grad.shape[0]
        down_grad[...] = value[:rows]
        up_grad[...] = value[rows:].T
    core = lax.axis_index("seq")
    half = own.shape[1]
    for c, term in ((core, own[...]), (1 - core, away[...].astype(F32))):
        columns = pl.ds(pl.multiple_of(c * half, 128), half)
        update[:, columns] = (term + dot(act[...], up[:, columns])).astype(BF16)


def finish_kernel(grouped, groups, *refs):
    count = len(groups)
    dq_parts, owns, aways = refs[:count], refs[count : 2 * count], refs[2 * count : 3 * count]
    dq, dk, dv = refs[3 * count :]
    places, _ = batch_places(grouped)
    width = dq.shape[1] // BATCHES
    for g, numbers in enumerate(groups):
        for i, number in enumerate(numbers):
            place = pl.ds(pl.multiple_of(places[number] * width, 128), width)
            o = slice(i * width, (i + 1) * width)
            dq[:, place] = dq_parts[g][:, o]
            for j, target in enumerate((dk, dv)):
                value = owns[g][j, :, o] + aways[g][j, :, o].astype(F32)
                target[:, place] = (value * FACTOR if j == 0 else value).astype(BF16)


VMEM = pl.BlockSpec(memory_space=pltpu.VMEM)
ANY = pl.BlockSpec(memory_space=pl.ANY)
HBM = pl.BlockSpec(memory_space=pltpu.HBM)


def shape(dims, dtype=BF16):
    return jax.ShapeDtypeStruct(dims, dtype)


def call(kernel, args, outs, in_specs, scratch, cost, megabytes):
    name = getattr(kernel, "func", kernel).__name__
    return pl.pallas_call(
        kernel,
        name=name,
        out_shape=outs,
        in_specs=in_specs,
        out_specs=[VMEM] * len(outs),
        scratch_shapes=scratch,
        compiler_params=pltpu.CompilerParams(vmem_limit_bytes=megabytes * 2**20),
        cost_estimate=pl.CostEstimate(flops=int(cost * 1e9), bytes_accessed=int(cost * 1e3), transcendentals=0),
    )(*args)


def local(
    queries,
    image_keys,
    image_values,
    text_keys,
    text_values,
    control_hint,
    proj_out,
    adapter_down,
    adapter_up,
    cotangent,
):
    shards = lax.axis_size("fsdp")
    grouped = shards == 8 and lax.axis_size("rep") == 2 and lax.axis_size("seq") == 2
    q, ko, vo = queries[0], image_keys[0], image_values[0]
    kt, vt, hint, cot = text_keys[0], text_values[0], control_hint[0], cotangent[0]
    rows, inner = q.shape
    wide = cot.shape[1]
    half = proj_out.shape[1]
    rank = hint.shape[1]
    depth = inner // (2 * BATCHES)
    width = 2 * depth
    core = lax.axis_index("seq")
    scale = float(shards * lax.axis_size("seq") * rows) ** (-0.5)

    kf, vf = swap(ko, "seq", 1), swap(vo, "seq", 1)
    cot_far = swap(lax.dynamic_slice_in_dim(cot, (1 - core) * half, half, 1), "seq", 1)
    (attn,) = call(
        forward_kernel,
        (q, ko, kf, kt, vo, vf, vt),
        [shape((rows, inner))],
        [HBM, HBM, ANY, HBM, HBM, ANY, HBM],
        [
            pltpu.VMEM((rows, inner), BF16),
            pltpu.VMEM((3 * rows, inner), BF16),
            pltpu.VMEM((3 * rows, inner), BF16),
            pltpu.SemaphoreType.DMA((3, 3)),
        ],
        0.119135,
        16,
    )
    if grouped:
        (message,) = call(
            pack_kernel,
            (proj_out, adapter_down, adapter_up),
            [shape((depth + 48, half))],
            [HBM] * 3,
            [
                pltpu.VMEM(adapter_down.shape, BF16),
                pltpu.VMEM(adapter_up.shape, BF16),
                pltpu.SemaphoreType.DMA((3,)),
            ],
            8.53264,
            16,
        )
        z1, x1 = ring_step(message), swap(message, "fsdp", 1)
        z1, x1, attn, cot_far = lax.optimization_barrier((z1, x1, attn, cot_far))
        z2, x2, y1 = ring_step(z1), swap(z1, "fsdp", 1), swap(z1, "rep", 1)
        end_x, end_y = ring_step(z1[depth:], turn=1), ring_step(x1[depth:], back=True)
    else:
        half_out = lax.all_gather(proj_out, "fsdp", axis=0, tiled=True)
        pieces = [half_out[i * depth : (i + 1) * depth] for i in range(2 * BATCHES)]
        adapters = (
            lax.all_gather(adapter_down, "fsdp", axis=0, tiled=True),
            lax.all_gather(adapter_up, "fsdp", axis=1, tiled=True),
        )
    attn_far = swap(attn, "seq", 1)

    def project(numbers, pieces, *carried):
        count = len(numbers)
        done = sum(numbers) if numbers == (1,) else 0
        outs = [shape((rows, (count + done) * width), F32), shape((rows, (count + done) * width))]
        if numbers[-1] == BATCHES - 1:
            outs += [shape((rows, half), F32), shape((rows, half))]
        else:
            outs += [shape((2 * rows, half), F32)]
        args = (*pieces, attn, attn_far, cot, cot_far, *carried)
        return call(
            functools.partial(project_kernel, grouped, numbers),
            args,
            outs,
            [ANY] * (2 * count) + [VMEM] * (len(args) - 2 * count),
            [pltpu.VMEM((count, width, half), BF16), pltpu.SemaphoreType.DMA((2 * count,))],
            (0.668445, 15.5525, 0.0371933, 0.0320126)[numbers[-1]],
            24,
        )

    near, far, total = project((0,), [message, x1] if grouped else pieces[:2])
    if grouped:
        z2, x2, y1, total = lax.optimization_barrier((z2, x2, y1, total))
        x3, y2 = swap(z2[:depth], "fsdp", 1), swap(x2[:depth], "rep", 1)
        pieces = [message, x1, z1, x2, y1, y2, z2, x3]
        adapters = (message, x1, z1, x2, y1, end_y, z2, end_x)
    outs = [
        shape((inner, rank)),
        shape((rank, wide)),
        shape((rows, rank)),
        shape((rows, rank)),
    ]
    if grouped:
        outs += [shape((8, 288, rank), F32), shape((8, 288, rank))]
        scratch = [
            pltpu.VMEM((inner + wide, rank), F32),
            pltpu.VMEM((8, 48, half), BF16),
            pltpu.SemaphoreType.DMA((8,)),
        ]
    else:
        outs += [shape((inner, rank), F32), shape((wide, rank), F32)]
        scratch = [pltpu.SemaphoreType.DMA((2,))]
    down, up, act, act_grad, first_term, second_term = call(
        functools.partial(adapter_kernel, grouped, scale),
        (*adapters, attn, cot, hint),
        outs,
        [ANY] * len(adapters) + [VMEM] * 3,
        scratch,
        8.73854,
        24,
    )
    def backward(numbers, near, far):
        count = len(numbers)
        return call(
            functools.partial(backward_kernel, grouped, numbers),
            (q, ko, kf, kt, vo, vf, vt, attn, near, far, act_grad, down),
            [
                shape((rows, count * width)),
                shape((2, rows, count * width), F32),
                shape((2, rows, count * width)),
            ],
            [HBM, HBM, ANY, HBM, HBM, ANY, HBM, ANY] + [VMEM] * 3 + [ANY],
            [
                pltpu.VMEM((count, rows, width), BF16),
                pltpu.VMEM((count, 3 * rows, width), BF16),
                pltpu.VMEM((count, 3 * rows, width), BF16),
                pltpu.VMEM((count, rows, width), BF16),
                pltpu.VMEM((count, width, rank), BF16),
                pltpu.SemaphoreType.DMA((count, 9)),
            ],
            (43.2055, 43.2055, 32.5195, 0.0437518)[numbers[-1]],
            16,
        )

    groups = ((0, 1), (2,), (3,))
    near, far, total = project((1,), pieces[2:4], near, far, total)
    far = swap(far, "seq", 1)
    if grouped:
        term = first_term + swap(second_term, "seq", 1).astype(F32)
        for mask in (2, 4):
            keep = term.shape[0] // 2
            term = term[:keep] + swap(term[keep:].astype(BF16), "fsdp", mask).astype(F32)
        term_far = swap(term[1].astype(BF16), "fsdp", 1)
    dq_a, own_a, away_a = backward(groups[0], near, far)
    away_a = swap(away_a, "seq", 1)
    if grouped:
        pieces[5], pieces[7], near = lax.optimization_barrier((pieces[5], pieces[7], near))
    near_b, far_b, total = project((2,), pieces[4:6], total)
    far_b = swap(far_b, "seq", 1)
    near_c, far_c, own_update, away_update = project((3,), pieces[6:8], total)
    far_c = swap(far_c, "seq", 1)
    away_update = swap(away_update, "seq", 1)
    if grouped:
        near_b, dq_a = lax.optimization_barrier((near_b, dq_a))
    dq_b, own_b, away_b = backward(groups[1], near_b, far_b)
    away_b = swap(away_b, "seq", 1)
    near_c, dq_b = lax.optimization_barrier((near_c, dq_b))
    dq_c, own_c, away_c = backward(groups[2], near_c, far_c)
    away_c = swap(away_c, "seq", 1)
    if not grouped:
        down_grad = lax.psum_scatter(first_term, ("fsdp", "seq"), scatter_dimension=0, tiled=True)
        up_grad = lax.psum_scatter(second_term, ("fsdp", "seq"), scatter_dimension=0, tiled=True).T
    args = [own_update, away_update, act, up]
    outs = [shape((rows, wide))]
    if grouped:
        args += [term, term_far]
        outs += [shape((96, rank), F32), shape((rank, 192), F32)]
    update, *adapter_grads = call(
        update_kernel, tuple(args), outs, [VMEM] * len(args), [], 7.44686, 24
    )
    if grouped:
        down_grad, up_grad = adapter_grads
    args = (dq_a, dq_b, dq_c, own_a, own_b, own_c, away_a, away_b, away_c)
    query_grad, key_grad, value_grad = call(
        functools.partial(finish_kernel, grouped, groups),
        args,
        [shape((rows, inner))] * 3,
        [VMEM] * len(args),
        [],
        44.0671,
        24,
    )
    return (update[None], query_grad[None], key_grad[None], value_grad[None], down_grad, up_grad)


def solution(mesh):
    rows = P(("rep", "fsdp"), "seq", None)
    text = P(("rep", "fsdp"), None, None)
    return jax.shard_map(
        local,
        mesh=mesh,
        in_specs=(
            rows,
            rows,
            rows,
            text,
            text,
            rows,
            P("fsdp", "seq"),
            P("fsdp", None),
            P(None, "fsdp"),
            rows,
        ),
        out_specs=(rows, rows, rows, rows, P(("rep", "fsdp", "seq"), None), P("rep", ("fsdp", "seq"))),
        check_vma=False,
    )
```

```python
import functools

import jax
import jax.numpy as jnp
from jax import lax
from jax.experimental import pallas as pl
from jax.experimental.pallas import tpu as pltpu
from jax.sharding import PartitionSpec as P

HD = 128
BATCHES = 4
FACTOR = HD ** (-0.5)
F32 = jnp.float32
BF16 = jnp.bfloat16
ROWS = (((0,), (0,)), ((), ()))
COLS = (((1,), (1,)), ((), ()))


def swap(value, axis, mask):
    pairs = [(source, source ^ mask) for source in range(lax.axis_size(axis))]
    return lax.ppermute(value, axis, pairs)


def ring_after(z):
    low, high = z % 2, z // 2
    return 2 * low + (1 - high)


def ring_before(z):
    low, high = z % 2, z // 2
    return 2 * (1 - low) + high


def ring_step(value, back=False, turn=0):
    pairs = []
    for f in range(8):
        z, x = f // 2, (f % 2) ^ turn
        pairs.append((f, ring_after(z) * 2 + x))
        pairs.append((8 + f, 8 + ring_before(z) * 2 + x))
    if back:
        pairs = [(target, source) for source, target in pairs]
    return lax.ppermute(value, ("rep", "fsdp"), pairs)


def dot(a, b, dims=None):
    if dims is None:
        return jnp.dot(a, b, preferred_element_type=F32)
    return lax.dot_general(a, b, dims, preferred_element_type=F32)


def batch_places(grouped):
    if not grouped:
        return list(range(BATCHES)), 0
    f = lax.axis_index("fsdp")
    rep = lax.axis_index("rep")
    z, x = f // 2, f % 2
    after, before = ring_after(z), ring_before(z)
    first = jnp.where(rep == 0, before, after)
    second = jnp.where(rep == 0, after, before)
    return [z, first, second, 3 - z], x


def softmax_parts(q, k):
    scores = dot(q, k, COLS) * FACTOR
    top = jnp.max(scores, -1, keepdims=True)
    weight = jnp.exp(scores - top)
    return weight * (1.0 / jnp.sum(weight, -1, keepdims=True))


def start_all(copies):
    for copy in copies:
        copy.start()


def forward_kernel(q_in, ko, kf, kt, vo, vf, vt, attn, q, keys, values, sems):
    rows, inner = q.shape
    copies = [pltpu.make_async_copy(q_in, q, sems.at[2, 0])]
    copies += [
        pltpu.make_async_copy(source, target.at[pl.ds(i * rows, rows)], sems.at[j, i])
        for j, (sources, target) in enumerate((((ko, kf, kt), keys), ((vo, vf, vt), values)))
        for i, source in enumerate(sources)
    ]
    start_all(copies)
    for copy in copies:
        copy.wait()
    for h in range(inner // HD):
        c = slice(h * HD, (h + 1) * HD)
        prob = softmax_parts(q[:, c], keys[:, c]).astype(BF16)
        attn[:, c] = dot(prob, values[:, c]).astype(BF16)


def pack_kernel(proj, down_in, up_in, message, down, up, sems):
    depth = proj.shape[0]
    copies = [
        pltpu.make_async_copy(down_in, down, sems.at[0]),
        pltpu.make_async_copy(up_in, up, sems.at[1]),
        pltpu.make_async_copy(proj, message.at[pl.ds(0, depth)], sems.at[2]),
    ]
    start_all(copies)
    copies[0].wait()
    copies[1].wait()
    for j in range(12):
        c = slice(128 * j, 128 * j + 128)
        message[depth : depth + 16, c] = down[16 * j : 16 * j + 16]
        a, b = j // 3, j % 3
        message[depth + 16 : depth + 48, c] = up[32 * a : 32 * a + 32, 128 * b : 128 * b + 128]
    copies[2].wait()


def adapter_kernel(packed, scale, *refs):
    if packed:
        sources, refs = refs[:8], refs[8:]
        (attn, cot, hint, down, up, act, act_grad, near, far, terms, messages, sems) = refs
        f = lax.axis_index("fsdp")
        core = lax.axis_index("seq")
        places, x = batch_places(True)
        copies = []
        for i, source in enumerate(sources):
            behind = source.shape[0] - 48
            copies.append(pltpu.make_async_copy(source.at[pl.ds(behind, 48)], messages.at[i], sems.at[i]))
        start_all(copies)
        for i, copy in enumerate(copies):
            copy.wait()
            block = places[i // 2] * 2 + (x if i % 2 == 0 else 1 - x)
            for j in range(12):
                c = slice(128 * j, 128 * j + 128)
                down[pl.ds(pl.multiple_of(block * 192 + 16 * j, 16), 16)] = messages[i, 0:16, c]
                a, b = j // 3, j % 3
                columns = pl.ds(pl.multiple_of(block * 384 + 128 * b, 128), 128)
                up[32 * a : 32 * a + 32, columns] = messages[i, 16:48, c]
    else:
        (down_in, up_in, attn, cot, hint, down, up, act, act_grad, down_term, up_term, sems) = refs
        copies = [
            pltpu.make_async_copy(down_in, down, sems.at[0]),
            pltpu.make_async_copy(up_in, up, sems.at[1]),
        ]
        start_all(copies)
        for copy in copies:
            copy.wait()
    pre_act = dot(attn[...], down[...]) + hint[...].astype(F32)
    logistic = 1.0 / (1.0 + jnp.exp(-pre_act))
    act[...] = (pre_act * logistic).astype(BF16)
    act_back = dot(cot[...], up[...], COLS)
    act_grad[...] = (act_back * logistic * (1.0 + pre_act * (1.0 - logistic))).astype(BF16)
    inner, wide = attn.shape[1], cot.shape[1]
    if not packed:
        down_term[...] = dot(attn[...], act_grad[...], ROWS) * scale
        up_term[...] = dot(cot[...], act[...], ROWS) * scale
        return
    terms[pl.ds(0, inner)] = dot(attn[...], act_grad[...], ROWS) * scale
    terms[pl.ds(inner, wide)] = dot(cot[...], act[...], ROWS) * scale
    for place, mask in enumerate((0, 4, 1, 5, 2, 6, 3, 7)):
        block = f ^ mask
        for target, half in ((near, core), (far, 1 - core)):
            piece = block * 2 + half
            rows = terms[pl.ds(pl.multiple_of(piece * 96, 32), 96)]
            target[place, 0:96] = rows.astype(target.dtype)
            rows = terms[pl.ds(pl.multiple_of(inner + piece * 192, 64), 192)]
            target[place, 96:288] = rows.astype(target.dtype)


def project_kernel(grouped, numbers, *refs):
    count = len(numbers)
    pieces = refs[: 2 * count]
    attn_own, attn_far, cot, cot_far = refs[2 * count : 2 * count + 4]
    rest = refs[2 * count + 4 :]
    carried = ()
    if numbers == (1,):
        carried, rest = rest[:2], rest[2:]
    total_in = None
    if numbers[0] > 0:
        total_in, rest = rest[0], rest[1:]
    last = numbers[-1] == BATCHES - 1
    if last:
        near, far, own, away, weights, sems = rest
    else:
        near, far, total, weights, sems = rest
    places, x = batch_places(grouped)
    core = lax.axis_index("seq")
    rows = attn_own.shape[0]
    depth = attn_own.shape[1] // (2 * BATCHES)
    half = pieces[0].shape[1]
    copies = []
    for i in range(count):
        for j in range(2):
            where = (x if j == 0 else 1 - x) * depth
            copies.append(
                pltpu.make_async_copy(
                    pieces[2 * i + j].at[pl.ds(0, depth)],
                    weights.at[i, pl.ds(where if isinstance(x, int) else pl.multiple_of(where, 32), depth)],
                    sems.at[2 * i + j],
                )
            )
    start_all(copies)
    columns = pl.ds(pl.multiple_of(core * half, 128), half)
    cot_rows = jnp.concatenate([cot[:, columns], cot_far[...]], 0)
    total_now = total_in[...] if total_in is not None else None
    base = 0
    if carried:
        base = carried[0].shape[1]
        near[:, :base] = carried[0][...]
        far[:, :base] = carried[1][...]
    for i, number in enumerate(numbers):
        for copy in copies[2 * i : 2 * i + 2]:
            copy.wait()
        back = dot(cot_rows, weights[i], COLS)
        span = slice(base + i * 2 * depth, base + (i + 1) * 2 * depth)
        near[:, span] = back[:rows]
        far[:, span] = back[rows:].astype(BF16)
        place = pl.ds(pl.multiple_of(places[number] * 2 * depth, 128), 2 * depth)
        attn_rows = jnp.concatenate([attn_own[:, place], attn_far[:, place]], 0)
        term = dot(attn_rows, weights[i])
        total_now = term if total_now is None else total_now + term
    if last:
        own[...] = total_now[:rows]
        away[...] = total_now[rows:].astype(BF16)
    else:
        total[...] = total_now


def backward_kernel(grouped, numbers, *refs):
    (q, ko, kf, kt, vo, vf, vt, attn, near, far, act_grad, down) = refs[:12]
    dq, own, away, qs, keys, values, attns, downs, sems = refs[12:]
    count = len(numbers)
    rows = q.shape[0]
    width = qs.shape[2]
    places, _ = batch_places(grouped)
    copies = []
    for i, number in enumerate(numbers):
        place = pl.ds(pl.multiple_of(places[number] * width, 128), width)
        moves = [(q.at[:, place], qs.at[i]), (attn.at[:, place], attns.at[i])]
        moves.append((down.at[place], downs.at[i]))
        for j, (k, v) in enumerate(((ko, vo), (kf, vf), (kt, vt))):
            moves.append((k.at[:, place], keys.at[i, pl.ds(j * rows, rows)]))
            moves.append((v.at[:, place], values.at[i, pl.ds(j * rows, rows)]))
        group = [
            pltpu.make_async_copy(source, target, sems.at[i, j])
            for j, (source, target) in enumerate(moves)
        ]
        start_all(group)
        copies.append(group)
    for i in range(count):
        for copy in copies[i]:
            copy.wait()
        span = slice(i * width, (i + 1) * width)
        grad = (near[:, span] + far[:, span].astype(F32) + dot(act_grad[...], downs[i], COLS)).astype(BF16)
        for h in range(width // HD):
            c = slice(h * HD, (h + 1) * HD)
            o = slice(i * width + h * HD, i * width + (h + 1) * HD)
            prob = softmax_parts(qs[i, :, c], keys[i, :, c])
            prob_half = prob.astype(BF16)
            head = grad[:, c]
            delta = jnp.sum(head.astype(F32) * attns[i, :, c].astype(F32), -1, keepdims=True)
            prob_grad = dot(head, values[i, :, c], COLS)
            score_grad = (prob * (prob_grad - delta)).astype(BF16)
            dq[:, o] = (dot(score_grad, keys[i, :, c]) * FACTOR).astype(BF16)
            key_term = dot(score_grad[:, : 2 * rows], qs[i, :, c], ROWS)
            value_term = dot(prob_half[:, : 2 * rows], head, ROWS)
            own[0, :, o] = key_term[:rows]
            own[1, :, o] = value_term[:rows]
            away[0, :, o] = key_term[rows:].astype(BF16)
            away[1, :, o] = value_term[rows:].astype(BF16)


def update_kernel(own, away, act, up, *refs):
    if len(refs) == 1:
        (update,) = refs
    else:
        term, term_far, update, down_grad, up_grad = refs
        value = term[0] + term_far[...].astype(F32)
        rows = down_grad.shape[0]
        down_grad[...] = value[:rows]
        up_grad[...] = value[rows:]
    core = lax.axis_index("seq")
    half = own.shape[1]
    for c, term in ((core, own[...]), (1 - core, away[...].astype(F32))):
        columns = pl.ds(pl.multiple_of(c * half, 128), half)
        update[:, columns] = (term + dot(act[...], up[:, columns])).astype(BF16)


def finish_kernel(grouped, groups, *refs):
    count = len(groups)
    dq_parts, owns, aways = refs[:count], refs[count : 2 * count], refs[2 * count : 3 * count]
    dq, dk, dv = refs[3 * count :]
    places, _ = batch_places(grouped)
    width = dq.shape[1] // BATCHES
    for g, numbers in enumerate(groups):
        for i, number in enumerate(numbers):
            place = pl.ds(pl.multiple_of(places[number] * width, 128), width)
            o = slice(i * width, (i + 1) * width)
            dq[:, place] = dq_parts[g][:, o]
            for j, target in enumerate((dk, dv)):
                value = owns[g][j, :, o] + aways[g][j, :, o].astype(F32)
                target[:, place] = (value * FACTOR if j == 0 else value).astype(BF16)


VMEM = pl.BlockSpec(memory_space=pltpu.VMEM)
ANY = pl.BlockSpec(memory_space=pl.ANY)
HBM = pl.BlockSpec(memory_space=pltpu.HBM)


def shape(dims, dtype=BF16):
    return jax.ShapeDtypeStruct(dims, dtype)


def call(kernel, args, outs, in_specs, scratch, cost, megabytes):
    name = getattr(kernel, "func", kernel).__name__
    return pl.pallas_call(
        kernel,
        name=name,
        out_shape=outs,
        in_specs=in_specs,
        out_specs=[VMEM] * len(outs),
        scratch_shapes=scratch,
        compiler_params=pltpu.CompilerParams(vmem_limit_bytes=megabytes * 2**20),
        cost_estimate=pl.CostEstimate(flops=int(cost * 1e9), bytes_accessed=int(cost * 1e3), transcendentals=0),
    )(*args)


def local(
    queries,
    image_keys,
    image_values,
    text_keys,
    text_values,
    control_hint,
    proj_out,
    adapter_down,
    adapter_up,
    cotangent,
):
    shards = lax.axis_size("fsdp")
    grouped = shards == 8 and lax.axis_size("rep") == 2 and lax.axis_size("seq") == 2
    q, ko, vo = queries[0], image_keys[0], image_values[0]
    kt, vt, hint, cot = text_keys[0], text_values[0], control_hint[0], cotangent[0]
    rows, inner = q.shape
    wide = cot.shape[1]
    half = proj_out.shape[1]
    rank = hint.shape[1]
    depth = inner // (2 * BATCHES)
    width = 2 * depth
    core = lax.axis_index("seq")
    scale = float(shards * lax.axis_size("seq") * rows) ** (-0.5)

    kf, vf = swap(ko, "seq", 1), swap(vo, "seq", 1)
    cot_far = swap(lax.dynamic_slice_in_dim(cot, (1 - core) * half, half, 1), "seq", 1)
    (attn,) = call(
        forward_kernel,
        (q, ko, kf, kt, vo, vf, vt),
        [shape((rows, inner))],
        [HBM, HBM, ANY, HBM, HBM, ANY, HBM],
        [
            pltpu.VMEM((rows, inner), BF16),
            pltpu.VMEM((3 * rows, inner), BF16),
            pltpu.VMEM((3 * rows, inner), BF16),
            pltpu.SemaphoreType.DMA((3, 3)),
        ],
        0.119135,
        16,
    )
    if grouped:
        (message,) = call(
            pack_kernel,
            (proj_out, adapter_down, adapter_up),
            [shape((depth + 48, half))],
            [HBM] * 3,
            [
                pltpu.VMEM(adapter_down.shape, BF16),
                pltpu.VMEM(adapter_up.shape, BF16),
                pltpu.SemaphoreType.DMA((3,)),
            ],
            8.53264,
            60,
        )
        z1, x1 = ring_step(message), swap(message, "fsdp", 1)
        z1, x1, attn, cot_far = lax.optimization_barrier((z1, x1, attn, cot_far))
        z2, x2, y1 = ring_step(z1), swap(z1, "fsdp", 1), swap(z1, "rep", 1)
        end_x, end_y = ring_step(z1[depth:], turn=1), ring_step(x1[depth:], back=True)
    else:
        half_out = lax.all_gather(proj_out, "fsdp", axis=0, tiled=True)
        pieces = [half_out[i * depth : (i + 1) * depth] for i in range(2 * BATCHES)]
        adapters = (
            lax.all_gather(adapter_down, "fsdp", axis=0, tiled=True),
            lax.all_gather(adapter_up, "fsdp", axis=1, tiled=True),
        )
    attn_far = swap(attn, "seq", 1)

    def project(numbers, pieces, *carried):
        count = len(numbers)
        done = sum(numbers) if numbers == (1,) else 0
        outs = [shape((rows, (count + done) * width), F32), shape((rows, (count + done) * width))]
        if numbers[-1] == BATCHES - 1:
            outs += [shape((rows, half), F32), shape((rows, half))]
        else:
            outs += [shape((2 * rows, half), F32)]
        args = (*pieces, attn, attn_far, cot, cot_far, *carried)
        return call(
            functools.partial(project_kernel, grouped, numbers),
            args,
            outs,
            [ANY] * (2 * count) + [VMEM] * (len(args) - 2 * count),
            [pltpu.VMEM((count, width, half), BF16), pltpu.SemaphoreType.DMA((2 * count,))],
            (0.668445, 15.5525, 0.0371933, 0.0320126)[numbers[-1]],
            24,
        )

    near, far, total = project((0,), [message, x1] if grouped else pieces[:2])
    if grouped:
        z2, x2, y1, total = lax.optimization_barrier((z2, x2, y1, total))
        x3, y2 = swap(z2[:depth], "fsdp", 1), swap(x2[:depth], "rep", 1)
        pieces = [message, x1, z1, x2, y1, y2, z2, x3]
        adapters = (message, x1, z1, x2, y1, end_y, z2, end_x)
    outs = [
        shape((inner, rank)),
        shape((rank, wide)),
        shape((rows, rank)),
        shape((rows, rank)),
    ]
    if grouped:
        outs += [shape((8, 288, rank), F32), shape((8, 288, rank))]
        scratch = [
            pltpu.VMEM((inner + wide, rank), F32),
            pltpu.VMEM((8, 48, half), BF16),
            pltpu.SemaphoreType.DMA((8,)),
        ]
    else:
        outs += [shape((inner, rank), F32), shape((wide, rank), F32)]
        scratch = [pltpu.SemaphoreType.DMA((2,))]
    down, up, act, act_grad, first_term, second_term = call(
        functools.partial(adapter_kernel, grouped, scale),
        (*adapters, attn, cot, hint),
        outs,
        [ANY] * len(adapters) + [VMEM] * 3,
        scratch,
        8.73854,
        24,
    )
    def backward(numbers, near, far):
        count = len(numbers)
        return call(
            functools.partial(backward_kernel, grouped, numbers),
            (q, ko, kf, kt, vo, vf, vt, attn, near, far, act_grad, down),
            [
                shape((rows, count * width)),
                shape((2, rows, count * width), F32),
                shape((2, rows, count * width)),
            ],
            [HBM, HBM, ANY, HBM, HBM, ANY, HBM, ANY] + [VMEM] * 3 + [ANY],
            [
                pltpu.VMEM((count, rows, width), BF16),
                pltpu.VMEM((count, 3 * rows, width), BF16),
                pltpu.VMEM((count, 3 * rows, width), BF16),
                pltpu.VMEM((count, rows, width), BF16),
                pltpu.VMEM((count, width, rank), BF16),
                pltpu.SemaphoreType.DMA((count, 9)),
            ],
            (43.2055, 43.2055, 32.5195, 0.0437518)[numbers[-1]],
            16,
        )

    groups = ((0, 1), (2,), (3,))
    near, far, total = project((1,), pieces[2:4], near, far, total)
    far = swap(far, "seq", 1)
    if grouped:
        term = first_term + swap(second_term, "seq", 1).astype(F32)
        for mask in (2, 1):
            keep = term.shape[0] // 2
            term = term[:keep] + swap(term[keep:].astype(BF16), "fsdp", mask).astype(F32)
        term_far = swap(term[1].astype(BF16), "fsdp", 4)
    dq_a, own_a, away_a = backward(groups[0], near, far)
    away_a = swap(away_a, "seq", 1)
    if grouped:
        pieces[5], pieces[7], near = lax.optimization_barrier((pieces[5], pieces[7], near))
    near_b, far_b, total = project((2,), pieces[4:6], total)
    far_b = swap(far_b, "seq", 1)
    near_c, far_c, own_update, away_update = project((3,), pieces[6:8], total)
    far_c = swap(far_c, "seq", 1)
    away_update = swap(away_update, "seq", 1)
    if grouped:
        near_b, dq_a = lax.optimization_barrier((near_b, dq_a))
    dq_b, own_b, away_b = backward(groups[1], near_b, far_b)
    away_b = swap(away_b, "seq", 1)
    near_c, dq_b = lax.optimization_barrier((near_c, dq_b))
    dq_c, own_c, away_c = backward(groups[2], near_c, far_c)
    away_c = swap(away_c, "seq", 1)
    if not grouped:
        down_grad = lax.psum_scatter(first_term, ("fsdp", "seq"), scatter_dimension=0, tiled=True)
        up_grad = lax.psum_scatter(second_term, ("fsdp", "seq"), scatter_dimension=0, tiled=True).T
    args = [own_update, away_update, act, up]
    outs = [shape((rows, wide))]
    if grouped:
        args += [term, term_far]
        outs += [shape((96, rank), F32), shape((192, rank), F32)]
    update, *adapter_grads = call(
        update_kernel, tuple(args), outs, [VMEM] * len(args), [], 7.44686, 24
    )
    if grouped:
        down_grad, up_grad = adapter_grads[0], adapter_grads[1].T
    args = (dq_a, dq_b, dq_c, own_a, own_b, own_c, away_a, away_b, away_c)
    query_grad, key_grad, value_grad = call(
        functools.partial(finish_kernel, grouped, groups),
        args,
        [shape((rows, inner))] * 3,
        [VMEM] * len(args),
        [],
        44.0671,
        24,
    )
    return (update[None], query_grad[None], key_grad[None], value_grad[None], down_grad, up_grad)


def solution(mesh):
    rows = P(("rep", "fsdp"), "seq", None)
    text = P(("rep", "fsdp"), None, None)
    return jax.shard_map(
        local,
        mesh=mesh,
        in_specs=(
            rows,
            rows,
            rows,
            text,
            text,
            rows,
            P("fsdp", "seq"),
            P("fsdp", None),
            P(None, "fsdp"),
            rows,
        ),
        out_specs=(rows, rows, rows, rows, P(("rep", "fsdp", "seq"), None), P("rep", ("fsdp", "seq"))),
        check_vma=False,
    )
```

```python
import functools

import jax
import jax.numpy as jnp
from jax import lax
from jax.experimental import pallas as pl
from jax.experimental.pallas import tpu as pltpu
from jax.sharding import PartitionSpec as P

HD = 128
BATCHES = 4
FACTOR = HD ** (-0.5)
F32 = jnp.float32
BF16 = jnp.bfloat16
ROWS = (((0,), (0,)), ((), ()))
COLS = (((1,), (1,)), ((), ()))


def swap(value, axis, mask):
    pairs = [(source, source ^ mask) for source in range(lax.axis_size(axis))]
    return lax.ppermute(value, axis, pairs)


def ring_after(z):
    low, high = z % 2, z // 2
    return 2 * low + (1 - high)


def ring_before(z):
    low, high = z % 2, z // 2
    return 2 * (1 - low) + high


def ring_step(value, back=False, turn=0):
    pairs = []
    for f in range(8):
        z, x = f // 2, (f % 2) ^ turn
        pairs.append((f, ring_after(z) * 2 + x))
        pairs.append((8 + f, 8 + ring_before(z) * 2 + x))
    if back:
        pairs = [(target, source) for source, target in pairs]
    return lax.ppermute(value, ("rep", "fsdp"), pairs)


def dot(a, b, dims=None):
    if dims is None:
        return jnp.dot(a, b, preferred_element_type=F32)
    return lax.dot_general(a, b, dims, preferred_element_type=F32)


def batch_places(grouped):
    if not grouped:
        return list(range(BATCHES)), 0
    f = lax.axis_index("fsdp")
    rep = lax.axis_index("rep")
    z, x = f // 2, f % 2
    after, before = ring_after(z), ring_before(z)
    first = jnp.where(rep == 0, before, after)
    second = jnp.where(rep == 0, after, before)
    return [z, first, second, 3 - z], x


def softmax_parts(q, k):
    scores = dot(q, k, COLS) * FACTOR
    top = jnp.max(scores, -1, keepdims=True)
    weight = jnp.exp(scores - top)
    return weight * (1.0 / jnp.sum(weight, -1, keepdims=True))


def start_all(copies):
    for copy in copies:
        copy.start()


def forward_kernel(q_in, ko, kf, kt, vo, vf, vt, attn, q, keys, values, sems):
    rows, inner = q.shape
    copies = [pltpu.make_async_copy(q_in, q, sems.at[2, 0])]
    copies += [
        pltpu.make_async_copy(source, target.at[pl.ds(i * rows, rows)], sems.at[j, i])
        for j, (sources, target) in enumerate((((ko, kf, kt), keys), ((vo, vf, vt), values)))
        for i, source in enumerate(sources)
    ]
    start_all(copies)
    for copy in copies:
        copy.wait()
    for h in range(inner // HD):
        c = slice(h * HD, (h + 1) * HD)
        prob = softmax_parts(q[:, c], keys[:, c]).astype(BF16)
        attn[:, c] = dot(prob, values[:, c]).astype(BF16)


def pack_kernel(proj, down_in, up_in, message, down, up, sems):
    depth = proj.shape[0]
    copies = [
        pltpu.make_async_copy(down_in, down, sems.at[0]),
        pltpu.make_async_copy(up_in, up, sems.at[1]),
        pltpu.make_async_copy(proj, message.at[pl.ds(0, depth)], sems.at[2]),
    ]
    start_all(copies)
    copies[0].wait()
    copies[1].wait()
    for j in range(12):
        c = slice(128 * j, 128 * j + 128)
        message[depth : depth + 16, c] = down[16 * j : 16 * j + 16]
        a, b = j // 3, j % 3
        message[depth + 16 : depth + 48, c] = up[32 * a : 32 * a + 32, 128 * b : 128 * b + 128]
    copies[2].wait()


def adapter_kernel(packed, scale, *refs):
    if packed:
        sources, refs = refs[:8], refs[8:]
        (attn, cot, hint, down, up, act, act_grad, near, far, terms, messages, sems) = refs
        f = lax.axis_index("fsdp")
        core = lax.axis_index("seq")
        places, x = batch_places(True)
        copies = []
        for i, source in enumerate(sources):
            behind = source.shape[0] - 48
            copies.append(pltpu.make_async_copy(source.at[pl.ds(behind, 48)], messages.at[i], sems.at[i]))
        start_all(copies)
        for i, copy in enumerate(copies):
            copy.wait()
            block = places[i // 2] * 2 + (x if i % 2 == 0 else 1 - x)
            for j in range(12):
                c = slice(128 * j, 128 * j + 128)
                down[pl.ds(pl.multiple_of(block * 192 + 16 * j, 16), 16)] = messages[i, 0:16, c]
                a, b = j // 3, j % 3
                columns = pl.ds(pl.multiple_of(block * 384 + 128 * b, 128), 128)
                up[32 * a : 32 * a + 32, columns] = messages[i, 16:48, c]
    else:
        (down_in, up_in, attn, cot, hint, down, up, act, act_grad, down_term, up_term, sems) = refs
        copies = [
            pltpu.make_async_copy(down_in, down, sems.at[0]),
            pltpu.make_async_copy(up_in, up, sems.at[1]),
        ]
        start_all(copies)
        for copy in copies:
            copy.wait()
    pre_act = dot(attn[...], down[...]) + hint[...].astype(F32)
    logistic = 1.0 / (1.0 + jnp.exp(-pre_act))
    act[...] = (pre_act * logistic).astype(BF16)
    act_back = dot(cot[...], up[...], COLS)
    act_grad[...] = (act_back * logistic * (1.0 + pre_act * (1.0 - logistic))).astype(BF16)
    inner, wide = attn.shape[1], cot.shape[1]
    if not packed:
        down_term[...] = dot(attn[...], act_grad[...], ROWS) * scale
        up_term[...] = dot(cot[...], act[...], ROWS) * scale
        return
    terms[pl.ds(0, inner)] = dot(attn[...], act_grad[...], ROWS) * scale
    terms[pl.ds(inner, wide)] = dot(cot[...], act[...], ROWS) * scale
    for place, mask in enumerate((0, 4, 1, 5, 2, 6, 3, 7)):
        block = f ^ mask
        for target, half in ((near, core), (far, 1 - core)):
            piece = block * 2 + half
            rows = terms[pl.ds(pl.multiple_of(piece * 96, 32), 96)]
            target[place, 0:96] = rows.astype(target.dtype)
            rows = terms[pl.ds(pl.multiple_of(inner + piece * 192, 64), 192)]
            target[place, 96:288] = rows.astype(target.dtype)


def project_kernel(grouped, numbers, *refs):
    count = len(numbers)
    pieces = refs[: 2 * count]
    attn_own, attn_far, cot, cot_far = refs[2 * count : 2 * count + 4]
    rest = refs[2 * count + 4 :]
    carried = ()
    if numbers == (1,):
        carried, rest = rest[:2], rest[2:]
    total_in = None
    if numbers[0] > 0:
        total_in, rest = rest[0], rest[1:]
    last = numbers[-1] == BATCHES - 1
    if last:
        near, far, own, away, weights, sems = rest
    else:
        near, far, total, weights, sems = rest
    places, x = batch_places(grouped)
    core = lax.axis_index("seq")
    rows = attn_own.shape[0]
    depth = attn_own.shape[1] // (2 * BATCHES)
    half = pieces[0].shape[1]
    copies = []
    for i in range(count):
        for j in range(2):
            where = (x if j == 0 else 1 - x) * depth
            copies.append(
                pltpu.make_async_copy(
                    pieces[2 * i + j].at[pl.ds(0, depth)],
                    weights.at[i, pl.ds(where if isinstance(x, int) else pl.multiple_of(where, 32), depth)],
                    sems.at[2 * i + j],
                )
            )
    start_all(copies)
    columns = pl.ds(pl.multiple_of(core * half, 128), half)
    cot_rows = jnp.concatenate([cot[:, columns], cot_far[...]], 0)
    total_now = total_in[...] if total_in is not None else None
    base = 0
    if carried:
        base = carried[0].shape[1]
        near[:, :base] = carried[0][...]
        far[:, :base] = carried[1][...]
    for i, number in enumerate(numbers):
        for copy in copies[2 * i : 2 * i + 2]:
            copy.wait()
        back = dot(cot_rows, weights[i], COLS)
        span = slice(base + i * 2 * depth, base + (i + 1) * 2 * depth)
        near[:, span] = back[:rows]
        far[:, span] = back[rows:].astype(BF16)
        place = pl.ds(pl.multiple_of(places[number] * 2 * depth, 128), 2 * depth)
        attn_rows = jnp.concatenate([attn_own[:, place], attn_far[:, place]], 0)
        term = dot(attn_rows, weights[i])
        total_now = term if total_now is None else total_now + term
    if last:
        own[...] = total_now[:rows]
        away[...] = total_now[rows:].astype(BF16)
    else:
        total[...] = total_now


def backward_kernel(grouped, numbers, *refs):
    (q, ko, kf, kt, vo, vf, vt, attn, near, far, act_grad, down) = refs[:12]
    dq, own, away, qs, keys, values, attns, downs, sems = refs[12:]
    count = len(numbers)
    rows = q.shape[0]
    width = qs.shape[2]
    places, _ = batch_places(grouped)
    copies = []
    for i, number in enumerate(numbers):
        place = pl.ds(pl.multiple_of(places[number] * width, 128), width)
        moves = [(q.at[:, place], qs.at[i]), (attn.at[:, place], attns.at[i])]
        moves.append((down.at[place], downs.at[i]))
        for j, (k, v) in enumerate(((ko, vo), (kf, vf), (kt, vt))):
            moves.append((k.at[:, place], keys.at[i, pl.ds(j * rows, rows)]))
            moves.append((v.at[:, place], values.at[i, pl.ds(j * rows, rows)]))
        group = [
            pltpu.make_async_copy(source, target, sems.at[i, j])
            for j, (source, target) in enumerate(moves)
        ]
        start_all(group)
        copies.append(group)
    for i in range(count):
        for copy in copies[i]:
            copy.wait()
        span = slice(i * width, (i + 1) * width)
        grad = (near[:, span] + far[:, span].astype(F32) + dot(act_grad[...], downs[i], COLS)).astype(BF16)
        for h in range(width // HD):
            c = slice(h * HD, (h + 1) * HD)
            o = slice(i * width + h * HD, i * width + (h + 1) * HD)
            prob = softmax_parts(qs[i, :, c], keys[i, :, c])
            prob_half = prob.astype(BF16)
            head = grad[:, c]
            delta = jnp.sum(head.astype(F32) * attns[i, :, c].astype(F32), -1, keepdims=True)
            prob_grad = dot(head, values[i, :, c], COLS)
            score_grad = (prob * (prob_grad - delta)).astype(BF16)
            dq[:, o] = (dot(score_grad, keys[i, :, c]) * FACTOR).astype(BF16)
            key_term = dot(score_grad[:, : 2 * rows], qs[i, :, c], ROWS)
            value_term = dot(prob_half[:, : 2 * rows], head, ROWS)
            own[0, :, o] = key_term[:rows]
            own[1, :, o] = value_term[:rows]
            away[0, :, o] = key_term[rows:].astype(BF16)
            away[1, :, o] = value_term[rows:].astype(BF16)


def update_kernel(own, away, act, up, *refs):
    held, sems = refs[-2:]
    refs = refs[:-2]
    update = refs[0] if len(refs) == 1 else refs[2]
    core = lax.axis_index("seq")
    half = own.shape[1]
    copies = []
    for i, (c, term) in enumerate(((core, own), (1 - core, away))):
        for j in range(2):
            span = slice(j * half // 2, (j + 1) * half // 2)
            columns = pl.ds(pl.multiple_of(c * half + j * (half // 2), 128), half // 2)
            held[:, columns] = (term[:, span].astype(F32) + dot(act[...], up[:, columns])).astype(BF16)
            copies.append(
                pltpu.make_async_copy(held.at[:, columns], update.at[:, columns], sems.at[2 * i + j])
            )
            copies[-1].start()
    if len(refs) > 1:
        term, term_far, _, down_grad, up_grad = refs
        value = term[0] + term_far[...].astype(F32)
        rows = down_grad.shape[0]
        down_grad[...] = value[:rows]
        up_grad[...] = value[rows:]
    for copy in copies:
        copy.wait()


def finish_kernel(grouped, groups, *refs):
    count = len(groups)
    dq_parts, owns, aways = refs[:count], refs[count : 2 * count], refs[2 * count : 3 * count]
    dq, dk, dv = refs[3 * count :]
    places, _ = batch_places(grouped)
    width = dq.shape[1] // BATCHES
    for g, numbers in enumerate(groups):
        for i, number in enumerate(numbers):
            place = pl.ds(pl.multiple_of(places[number] * width, 128), width)
            o = slice(i * width, (i + 1) * width)
            dq[:, place] = dq_parts[g][:, o]
            for j, target in enumerate((dk, dv)):
                value = owns[g][j, :, o] + aways[g][j, :, o].astype(F32)
                target[:, place] = (value * FACTOR if j == 0 else value).astype(BF16)


VMEM = pl.BlockSpec(memory_space=pltpu.VMEM)
ANY = pl.BlockSpec(memory_space=pl.ANY)
HBM = pl.BlockSpec(memory_space=pltpu.HBM)


def shape(dims, dtype=BF16):
    return jax.ShapeDtypeStruct(dims, dtype)


def call(kernel, args, outs, in_specs, scratch, cost, megabytes, placed=None):
    name = getattr(kernel, "func", kernel).__name__
    return pl.pallas_call(
        kernel,
        name=name,
        out_shape=outs,
        in_specs=in_specs,
        out_specs=placed or [VMEM] * len(outs),
        scratch_shapes=scratch,
        compiler_params=pltpu.CompilerParams(vmem_limit_bytes=megabytes * 2**20),
        cost_estimate=pl.CostEstimate(flops=int(cost * 1e9), bytes_accessed=int(cost * 1e3), transcendentals=0),
    )(*args)


def local(
    queries,
    image_keys,
    image_values,
    text_keys,
    text_values,
    control_hint,
    proj_out,
    adapter_down,
    adapter_up,
    cotangent,
):
    shards = lax.axis_size("fsdp")
    grouped = shards == 8 and lax.axis_size("rep") == 2 and lax.axis_size("seq") == 2
    q, ko, vo = queries[0], image_keys[0], image_values[0]
    kt, vt, hint, cot = text_keys[0], text_values[0], control_hint[0], cotangent[0]
    rows, inner = q.shape
    wide = cot.shape[1]
    half = proj_out.shape[1]
    rank = hint.shape[1]
    depth = inner // (2 * BATCHES)
    width = 2 * depth
    core = lax.axis_index("seq")
    scale = float(shards * lax.axis_size("seq") * rows) ** (-0.5)

    kf, vf = swap(ko, "seq", 1), swap(vo, "seq", 1)
    cot_far = swap(lax.dynamic_slice_in_dim(cot, (1 - core) * half, half, 1), "seq", 1)
    (attn,) = call(
        forward_kernel,
        (q, ko, kf, kt, vo, vf, vt),
        [shape((rows, inner))],
        [HBM, HBM, ANY, HBM, HBM, ANY, HBM],
        [
            pltpu.VMEM((rows, inner), BF16),
            pltpu.VMEM((3 * rows, inner), BF16),
            pltpu.VMEM((3 * rows, inner), BF16),
            pltpu.SemaphoreType.DMA((3, 3)),
        ],
        0.119135,
        16,
    )
    if grouped:
        (message,) = call(
            pack_kernel,
            (proj_out, adapter_down, adapter_up),
            [shape((depth + 48, half))],
            [HBM] * 3,
            [
                pltpu.VMEM(adapter_down.shape, BF16),
                pltpu.VMEM(adapter_up.shape, BF16),
                pltpu.SemaphoreType.DMA((3,)),
            ],
            8.53264,
            60,
        )
        z1, x1 = ring_step(message), swap(message, "fsdp", 1)
        z1, x1, attn, cot_far = lax.optimization_barrier((z1, x1, attn, cot_far))
        z2, x2, y1 = ring_step(z1), swap(z1, "fsdp", 1), swap(z1, "rep", 1)
        end_x, end_y = ring_step(z1[depth:], turn=1), ring_step(x1[depth:], back=True)
    else:
        half_out = lax.all_gather(proj_out, "fsdp", axis=0, tiled=True)
        pieces = [half_out[i * depth : (i + 1) * depth] for i in range(2 * BATCHES)]
        adapters = (
            lax.all_gather(adapter_down, "fsdp", axis=0, tiled=True),
            lax.all_gather(adapter_up, "fsdp", axis=1, tiled=True),
        )
    attn_far = swap(attn, "seq", 1)

    def project(numbers, pieces, *carried):
        count = len(numbers)
        done = sum(numbers) if numbers == (1,) else 0
        outs = [shape((rows, (count + done) * width), F32), shape((rows, (count + done) * width))]
        if numbers[-1] == BATCHES - 1:
            outs += [shape((rows, half), F32), shape((rows, half))]
        else:
            outs += [shape((2 * rows, half), F32)]
        args = (*pieces, attn, attn_far, cot, cot_far, *carried)
        return call(
            functools.partial(project_kernel, grouped, numbers),
            args,
            outs,
            [ANY] * (2 * count) + [VMEM] * (len(args) - 2 * count),
            [pltpu.VMEM((count, width, half), BF16), pltpu.SemaphoreType.DMA((2 * count,))],
            (0.668445, 15.5525, 0.0371933, 0.0320126)[numbers[-1]],
            24,
        )

    near, far, total = project((0,), [message, x1] if grouped else pieces[:2])
    if grouped:
        z2, x2, y1, total = lax.optimization_barrier((z2, x2, y1, total))
        x3, y2 = swap(z2[:depth], "fsdp", 1), swap(x2[:depth], "rep", 1)
        pieces = [message, x1, z1, x2, y1, y2, z2, x3]
        adapters = (message, x1, z1, x2, y1, end_y, z2, end_x)
    outs = [
        shape((inner, rank)),
        shape((rank, wide)),
        shape((rows, rank)),
        shape((rows, rank)),
    ]
    if grouped:
        outs += [shape((8, 288, rank), F32), shape((8, 288, rank))]
        scratch = [
            pltpu.VMEM((inner + wide, rank), F32),
            pltpu.VMEM((8, 48, half), BF16),
            pltpu.SemaphoreType.DMA((8,)),
        ]
    else:
        outs += [shape((inner, rank), F32), shape((wide, rank), F32)]
        scratch = [pltpu.SemaphoreType.DMA((2,))]
    down, up, act, act_grad, first_term, second_term = call(
        functools.partial(adapter_kernel, grouped, scale),
        (*adapters, attn, cot, hint),
        outs,
        [ANY] * len(adapters) + [VMEM] * 3,
        scratch,
        8.73854,
        24,
    )
    def backward(numbers, near, far):
        count = len(numbers)
        return call(
            functools.partial(backward_kernel, grouped, numbers),
            (q, ko, kf, kt, vo, vf, vt, attn, near, far, act_grad, down),
            [
                shape((rows, count * width)),
                shape((2, rows, count * width), F32),
                shape((2, rows, count * width)),
            ],
            [HBM, HBM, ANY, HBM, HBM, ANY, HBM, ANY] + [VMEM] * 3 + [ANY],
            [
                pltpu.VMEM((count, rows, width), BF16),
                pltpu.VMEM((count, 3 * rows, width), BF16),
                pltpu.VMEM((count, 3 * rows, width), BF16),
                pltpu.VMEM((count, rows, width), BF16),
                pltpu.VMEM((count, width, rank), BF16),
                pltpu.SemaphoreType.DMA((count, 9)),
            ],
            (43.2055, 43.2055, 32.5195, 0.0437518)[numbers[-1]],
            16,
        )

    groups = ((0, 1), (2,), (3,))
    near, far, total = project((1,), pieces[2:4], near, far, total)
    far = swap(far, "seq", 1)
    if grouped:
        term = first_term + swap(second_term, "seq", 1).astype(F32)
        for mask in (2, 1):
            keep = term.shape[0] // 2
            term = term[:keep] + swap(term[keep:].astype(BF16), "fsdp", mask).astype(F32)
        term_far = swap(term[1].astype(BF16), "fsdp", 4)
    dq_a, own_a, away_a = backward(groups[0], near, far)
    away_a = swap(away_a, "seq", 1)
    if grouped:
        pieces[5], pieces[7], near = lax.optimization_barrier((pieces[5], pieces[7], near))
    near_b, far_b, total = project((2,), pieces[4:6], total)
    far_b = swap(far_b, "seq", 1)
    near_c, far_c, own_update, away_update = project((3,), pieces[6:8], total)
    far_c = swap(far_c, "seq", 1)
    away_update = swap(away_update, "seq", 1)
    if grouped:
        near_b, dq_a = lax.optimization_barrier((near_b, dq_a))
    dq_b, own_b, away_b = backward(groups[1], near_b, far_b)
    away_b = swap(away_b, "seq", 1)
    near_c, dq_b = lax.optimization_barrier((near_c, dq_b))
    dq_c, own_c, away_c = backward(groups[2], near_c, far_c)
    away_c = swap(away_c, "seq", 1)
    if not grouped:
        down_grad = lax.psum_scatter(first_term, ("fsdp", "seq"), scatter_dimension=0, tiled=True)
        up_grad = lax.psum_scatter(second_term, ("fsdp", "seq"), scatter_dimension=0, tiled=True).T
    args = [own_update, away_update, act, up]
    outs = [shape((rows, wide))]
    if grouped:
        args += [term, term_far]
        outs += [shape((96, rank), F32), shape((192, rank), F32)]
    update, *adapter_grads = call(
        update_kernel,
        tuple(args),
        outs,
        [VMEM] * len(args),
        [pltpu.VMEM((rows, wide), BF16), pltpu.SemaphoreType.DMA((4,))],
        7.44686,
        24,
        [HBM] + [VMEM] * (len(outs) - 1),
    )
    if grouped:
        down_grad, up_grad = adapter_grads[0], adapter_grads[1].T
    args = (dq_a, dq_b, dq_c, own_a, own_b, own_c, away_a, away_b, away_c)
    query_grad, key_grad, value_grad = call(
        functools.partial(finish_kernel, grouped, groups),
        args,
        [shape((rows, inner))] * 3,
        [VMEM] * len(args),
        [],
        44.0671,
        24,
    )
    return (update[None], query_grad[None], key_grad[None], value_grad[None], down_grad, up_grad)


def solution(mesh):
    rows = P(("rep", "fsdp"), "seq", None)
    text = P(("rep", "fsdp"), None, None)
    return jax.shard_map(
        local,
        mesh=mesh,
        in_specs=(
            rows,
            rows,
            rows,
            text,
            text,
            rows,
            P("fsdp", "seq"),
            P("fsdp", None),
            P(None, "fsdp"),
            rows,
        ),
        out_specs=(rows, rows, rows, rows, P(("rep", "fsdp", "seq"), None), P("rep", ("fsdp", "seq"))),
        check_vma=False,
    )
```

```python
import functools

import jax
import jax.numpy as jnp
from jax import lax
from jax.experimental import pallas as pl
from jax.experimental.pallas import tpu as pltpu
from jax.sharding import PartitionSpec as P

HD = 128
BATCHES = 4
FACTOR = HD ** (-0.5)
F32 = jnp.float32
BF16 = jnp.bfloat16
ROWS = (((0,), (0,)), ((), ()))
COLS = (((1,), (1,)), ((), ()))


def swap(value, axis, mask):
    pairs = [(source, source ^ mask) for source in range(lax.axis_size(axis))]
    return lax.ppermute(value, axis, pairs)


def ring_after(z):
    low, high = z % 2, z // 2
    return 2 * low + (1 - high)


def ring_before(z):
    low, high = z % 2, z // 2
    return 2 * (1 - low) + high


def ring_step(value, back=False, turn=0):
    pairs = []
    for f in range(8):
        z, x = f // 2, (f % 2) ^ turn
        pairs.append((f, ring_after(z) * 2 + x))
        pairs.append((8 + f, 8 + ring_before(z) * 2 + x))
    if back:
        pairs = [(target, source) for source, target in pairs]
    return lax.ppermute(value, ("rep", "fsdp"), pairs)


def dot(a, b, dims=None):
    if dims is None:
        return jnp.dot(a, b, preferred_element_type=F32)
    return lax.dot_general(a, b, dims, preferred_element_type=F32)


def batch_places(grouped):
    if not grouped:
        return list(range(BATCHES)), 0
    f = lax.axis_index("fsdp")
    rep = lax.axis_index("rep")
    z, x = f // 2, f % 2
    after, before = ring_after(z), ring_before(z)
    first = jnp.where(rep == 0, before, after)
    second = jnp.where(rep == 0, after, before)
    return [z, first, second, 3 - z], x


def softmax_parts(q, k):
    scores = dot(q, k, COLS) * FACTOR
    top = jnp.max(scores, -1, keepdims=True)
    weight = jnp.exp(scores - top)
    return weight * (1.0 / jnp.sum(weight, -1, keepdims=True))


def start_all(copies):
    for copy in copies:
        copy.start()


def forward_kernel(q_in, ko, kf, kt, vo, vf, vt, attn, q, keys, values, sems):
    rows, inner = q.shape
    copies = [pltpu.make_async_copy(q_in, q, sems.at[2, 0])]
    copies += [
        pltpu.make_async_copy(source, target.at[pl.ds(i * rows, rows)], sems.at[j, i])
        for j, (sources, target) in enumerate((((ko, kf, kt), keys), ((vo, vf, vt), values)))
        for i, source in enumerate(sources)
    ]
    start_all(copies)
    for copy in copies:
        copy.wait()
    for h in range(inner // HD):
        c = slice(h * HD, (h + 1) * HD)
        prob = softmax_parts(q[:, c], keys[:, c]).astype(BF16)
        attn[:, c] = dot(prob, values[:, c]).astype(BF16)


def pack_kernel(proj, down_in, up_in, message, down, up, held, sems):
    depth = proj.shape[0]
    parts = [pl.ds(start, 48) for start in range(0, depth + 48, 48)]
    adapters = [
        pltpu.make_async_copy(down_in, down, sems.at[0, 0]),
        pltpu.make_async_copy(up_in, up, sems.at[0, 1]),
    ]
    copies = [
        pltpu.make_async_copy(proj.at[part], held.at[part], sems.at[1, i])
        for i, part in enumerate(parts[:-1])
    ]
    start_all(adapters + copies)
    for copy in adapters:
        copy.wait()
    for j in range(12):
        c = slice(128 * j, 128 * j + 128)
        held[depth : depth + 16, c] = down[16 * j : 16 * j + 16]
        a, b = j // 3, j % 3
        held[depth + 16 : depth + 48, c] = up[32 * a : 32 * a + 32, 128 * b : 128 * b + 128]
    away = [
        pltpu.make_async_copy(held.at[part], message.at[part], sems.at[2, i]) for i, part in enumerate(parts)
    ]
    away[-1].start()
    for copy, other in zip(copies, away):
        copy.wait()
        other.start()
    for other in away:
        other.wait()


def adapter_kernel(packed, scale, *refs):
    if packed:
        sources, refs = refs[:8], refs[8:]
        (attn, cot, hint, down, up, act, act_grad, near, far, terms, messages, sems) = refs
        f = lax.axis_index("fsdp")
        core = lax.axis_index("seq")
        places, x = batch_places(True)
        copies = []
        for i, source in enumerate(sources):
            behind = source.shape[0] - 48
            copies.append(pltpu.make_async_copy(source.at[pl.ds(behind, 48)], messages.at[i], sems.at[i]))
        start_all(copies)
        for i, copy in enumerate(copies):
            copy.wait()
            block = places[i // 2] * 2 + (x if i % 2 == 0 else 1 - x)
            for j in range(12):
                c = slice(128 * j, 128 * j + 128)
                down[pl.ds(pl.multiple_of(block * 192 + 16 * j, 16), 16)] = messages[i, 0:16, c]
                a, b = j // 3, j % 3
                columns = pl.ds(pl.multiple_of(block * 384 + 128 * b, 128), 128)
                up[32 * a : 32 * a + 32, columns] = messages[i, 16:48, c]
    else:
        (down_in, up_in, attn, cot, hint, down, up, act, act_grad, down_term, up_term, sems) = refs
        copies = [
            pltpu.make_async_copy(down_in, down, sems.at[0]),
            pltpu.make_async_copy(up_in, up, sems.at[1]),
        ]
        start_all(copies)
        for copy in copies:
            copy.wait()
    pre_act = dot(attn[...], down[...]) + hint[...].astype(F32)
    logistic = 1.0 / (1.0 + jnp.exp(-pre_act))
    act[...] = (pre_act * logistic).astype(BF16)
    act_back = dot(cot[...], up[...], COLS)
    act_grad[...] = (act_back * logistic * (1.0 + pre_act * (1.0 - logistic))).astype(BF16)
    inner, wide = attn.shape[1], cot.shape[1]
    if not packed:
        down_term[...] = dot(attn[...], act_grad[...], ROWS) * scale
        up_term[...] = dot(cot[...], act[...], ROWS) * scale
        return
    terms[pl.ds(0, inner)] = dot(attn[...], act_grad[...], ROWS) * scale
    terms[pl.ds(inner, wide)] = dot(cot[...], act[...], ROWS) * scale
    for place, mask in enumerate((0, 4, 1, 5, 2, 6, 3, 7)):
        block = f ^ mask
        for target, half in ((near, core), (far, 1 - core)):
            piece = block * 2 + half
            rows = terms[pl.ds(pl.multiple_of(piece * 96, 32), 96)]
            target[place, 0:96] = rows.astype(target.dtype)
            rows = terms[pl.ds(pl.multiple_of(inner + piece * 192, 64), 192)]
            target[place, 96:288] = rows.astype(target.dtype)


def project_kernel(grouped, numbers, *refs):
    count = len(numbers)
    pieces = refs[: 2 * count]
    attn_own, attn_far, cot, cot_far = refs[2 * count : 2 * count + 4]
    rest = refs[2 * count + 4 :]
    carried = ()
    if numbers == (1,):
        carried, rest = rest[:2], rest[2:]
    total_in = None
    if numbers[0] > 0:
        total_in, rest = rest[0], rest[1:]
    last = numbers[-1] == BATCHES - 1
    if last:
        near, far, own, away, weights, sems = rest
    else:
        near, far, total, weights, sems = rest
    places, x = batch_places(grouped)
    core = lax.axis_index("seq")
    rows = attn_own.shape[0]
    depth = attn_own.shape[1] // (2 * BATCHES)
    half = pieces[0].shape[1]
    copies = []
    for i in range(count):
        for j in range(2):
            where = (x if j == 0 else 1 - x) * depth
            copies.append(
                pltpu.make_async_copy(
                    pieces[2 * i + j].at[pl.ds(0, depth)],
                    weights.at[i, pl.ds(where if isinstance(x, int) else pl.multiple_of(where, 32), depth)],
                    sems.at[2 * i + j],
                )
            )
    start_all(copies)
    columns = pl.ds(pl.multiple_of(core * half, 128), half)
    cot_rows = jnp.concatenate([cot[:, columns], cot_far[...]], 0)
    total_now = total_in[...] if total_in is not None else None
    base = 0
    if carried:
        base = carried[0].shape[1]
        near[:, :base] = carried[0][...]
        far[:, :base] = carried[1][...]
    for i, number in enumerate(numbers):
        for copy in copies[2 * i : 2 * i + 2]:
            copy.wait()
        back = dot(cot_rows, weights[i], COLS)
        span = slice(base + i * 2 * depth, base + (i + 1) * 2 * depth)
        near[:, span] = back[:rows]
        far[:, span] = back[rows:].astype(BF16)
        place = pl.ds(pl.multiple_of(places[number] * 2 * depth, 128), 2 * depth)
        attn_rows = jnp.concatenate([attn_own[:, place], attn_far[:, place]], 0)
        term = dot(attn_rows, weights[i])
        total_now = term if total_now is None else total_now + term
    if last:
        own[...] = total_now[:rows]
        away[...] = total_now[rows:].astype(BF16)
    else:
        total[...] = total_now


def backward_kernel(grouped, numbers, *refs):
    (q, ko, kf, kt, vo, vf, vt, attn, near, far, act_grad, down) = refs[:12]
    dq, own, away, qs, keys, values, attns, downs, sems = refs[12:]
    count = len(numbers)
    rows = q.shape[0]
    width = qs.shape[2]
    places, _ = batch_places(grouped)
    copies = []
    for i, number in enumerate(numbers):
        place = pl.ds(pl.multiple_of(places[number] * width, 128), width)
        moves = [(q.at[:, place], qs.at[i]), (attn.at[:, place], attns.at[i])]
        moves.append((down.at[place], downs.at[i]))
        for j, (k, v) in enumerate(((ko, vo), (kf, vf), (kt, vt))):
            moves.append((k.at[:, place], keys.at[i, pl.ds(j * rows, rows)]))
            moves.append((v.at[:, place], values.at[i, pl.ds(j * rows, rows)]))
        group = [
            pltpu.make_async_copy(source, target, sems.at[i, j])
            for j, (source, target) in enumerate(moves)
        ]
        start_all(group)
        copies.append(group)
    for i in range(count):
        for copy in copies[i]:
            copy.wait()
        span = slice(i * width, (i + 1) * width)
        grad = (near[:, span] + far[:, span].astype(F32) + dot(act_grad[...], downs[i], COLS)).astype(BF16)
        for h in range(width // HD):
            c = slice(h * HD, (h + 1) * HD)
            o = slice(i * width + h * HD, i * width + (h + 1) * HD)
            prob = softmax_parts(qs[i, :, c], keys[i, :, c])
            prob_half = prob.astype(BF16)
            head = grad[:, c]
            delta = jnp.sum(head.astype(F32) * attns[i, :, c].astype(F32), -1, keepdims=True)
            prob_grad = dot(head, values[i, :, c], COLS)
            score_grad = (prob * (prob_grad - delta)).astype(BF16)
            dq[:, o] = (dot(score_grad, keys[i, :, c]) * FACTOR).astype(BF16)
            key_term = dot(score_grad[:, : 2 * rows], qs[i, :, c], ROWS)
            value_term = dot(prob_half[:, : 2 * rows], head, ROWS)
            own[0, :, o] = key_term[:rows]
            own[1, :, o] = value_term[:rows]
            away[0, :, o] = key_term[rows:].astype(BF16)
            away[1, :, o] = value_term[rows:].astype(BF16)


def update_kernel(own, away, act, up, *refs):
    if len(refs) == 1:
        (update,) = refs
    else:
        term, term_far, update, down_grad, up_grad = refs
        value = term[0] + term_far[...].astype(F32)
        rows = down_grad.shape[0]
        down_grad[...] = value[:rows]
        up_grad[...] = value[rows:]
    core = lax.axis_index("seq")
    half = own.shape[1]
    for c, term in ((core, own[...]), (1 - core, away[...].astype(F32))):
        columns = pl.ds(pl.multiple_of(c * half, 128), half)
        update[:, columns] = (term + dot(act[...], up[:, columns])).astype(BF16)


def finish_kernel(grouped, groups, *refs):
    count = len(groups)
    dq_parts, owns, aways = refs[:count], refs[count : 2 * count], refs[2 * count : 3 * count]
    dq, dk, dv = refs[3 * count :]
    places, _ = batch_places(grouped)
    width = dq.shape[1] // BATCHES
    for g, numbers in enumerate(groups):
        for i, number in enumerate(numbers):
            place = pl.ds(pl.multiple_of(places[number] * width, 128), width)
            o = slice(i * width, (i + 1) * width)
            dq[:, place] = dq_parts[g][:, o]
            for j, target in enumerate((dk, dv)):
                value = owns[g][j, :, o] + aways[g][j, :, o].astype(F32)
                target[:, place] = (value * FACTOR if j == 0 else value).astype(BF16)


VMEM = pl.BlockSpec(memory_space=pltpu.VMEM)
ANY = pl.BlockSpec(memory_space=pl.ANY)
HBM = pl.BlockSpec(memory_space=pltpu.HBM)


def shape(dims, dtype=BF16):
    return jax.ShapeDtypeStruct(dims, dtype)


def call(kernel, args, outs, in_specs, scratch, cost, megabytes, placed=None):
    name = getattr(kernel, "func", kernel).__name__
    return pl.pallas_call(
        kernel,
        name=name,
        out_shape=outs,
        in_specs=in_specs,
        out_specs=placed or [VMEM] * len(outs),
        scratch_shapes=scratch,
        compiler_params=pltpu.CompilerParams(vmem_limit_bytes=megabytes * 2**20),
        cost_estimate=pl.CostEstimate(flops=int(cost * 1e9), bytes_accessed=int(cost * 1e3), transcendentals=0),
    )(*args)


def local(
    queries,
    image_keys,
    image_values,
    text_keys,
    text_values,
    control_hint,
    proj_out,
    adapter_down,
    adapter_up,
    cotangent,
):
    shards = lax.axis_size("fsdp")
    grouped = shards == 8 and lax.axis_size("rep") == 2 and lax.axis_size("seq") == 2
    q, ko, vo = queries[0], image_keys[0], image_values[0]
    kt, vt, hint, cot = text_keys[0], text_values[0], control_hint[0], cotangent[0]
    rows, inner = q.shape
    wide = cot.shape[1]
    half = proj_out.shape[1]
    rank = hint.shape[1]
    depth = inner // (2 * BATCHES)
    width = 2 * depth
    core = lax.axis_index("seq")
    scale = float(shards * lax.axis_size("seq") * rows) ** (-0.5)

    kf, vf = swap(ko, "seq", 1), swap(vo, "seq", 1)
    cot_far = swap(lax.dynamic_slice_in_dim(cot, (1 - core) * half, half, 1), "seq", 1)
    (attn,) = call(
        forward_kernel,
        (q, ko, kf, kt, vo, vf, vt),
        [shape((rows, inner))],
        [HBM, HBM, ANY, HBM, HBM, ANY, HBM],
        [
            pltpu.VMEM((rows, inner), BF16),
            pltpu.VMEM((3 * rows, inner), BF16),
            pltpu.VMEM((3 * rows, inner), BF16),
            pltpu.SemaphoreType.DMA((3, 3)),
        ],
        0.119135,
        16,
    )
    if grouped:
        (message,) = call(
            pack_kernel,
            (proj_out, adapter_down, adapter_up),
            [shape((depth + 48, half))],
            [HBM] * 3,
            [
                pltpu.VMEM(adapter_down.shape, BF16),
                pltpu.VMEM(adapter_up.shape, BF16),
                pltpu.VMEM((depth + 48, half), BF16),
                pltpu.SemaphoreType.DMA((3, 5)),
            ],
            8.53264,
            60,
            [ANY],
        )
        z1, x1 = ring_step(message), swap(message, "fsdp", 1)
        z1, x1, attn, cot_far = lax.optimization_barrier((z1, x1, attn, cot_far))
        z2, x2, y1 = ring_step(z1), swap(z1, "fsdp", 1), swap(z1, "rep", 1)
        end_x, end_y = ring_step(z1[depth:], turn=1), ring_step(x1[depth:], back=True)
    else:
        half_out = lax.all_gather(proj_out, "fsdp", axis=0, tiled=True)
        pieces = [half_out[i * depth : (i + 1) * depth] for i in range(2 * BATCHES)]
        adapters = (
            lax.all_gather(adapter_down, "fsdp", axis=0, tiled=True),
            lax.all_gather(adapter_up, "fsdp", axis=1, tiled=True),
        )
    attn_far = swap(attn, "seq", 1)

    def project(numbers, pieces, *carried):
        count = len(numbers)
        done = sum(numbers) if numbers == (1,) else 0
        outs = [shape((rows, (count + done) * width), F32), shape((rows, (count + done) * width))]
        if numbers[-1] == BATCHES - 1:
            outs += [shape((rows, half), F32), shape((rows, half))]
        else:
            outs += [shape((2 * rows, half), F32)]
        args = (*pieces, attn, attn_far, cot, cot_far, *carried)
        return call(
            functools.partial(project_kernel, grouped, numbers),
            args,
            outs,
            [ANY] * (2 * count) + [VMEM] * (len(args) - 2 * count),
            [pltpu.VMEM((count, width, half), BF16), pltpu.SemaphoreType.DMA((2 * count,))],
            (0.668445, 15.5525, 0.0371933, 0.0320126)[numbers[-1]],
            18,
        )

    near, far, total = project((0,), [message, x1] if grouped else pieces[:2])
    if grouped:
        z2, x2, y1, total = lax.optimization_barrier((z2, x2, y1, total))
        x3, y2 = swap(z2[:depth], "fsdp", 1), swap(x2[:depth], "rep", 1)
        pieces = [message, x1, z1, x2, y1, y2, z2, x3]
        adapters = (message, x1, z1, x2, y1, end_y, z2, end_x)
    outs = [
        shape((inner, rank)),
        shape((rank, wide)),
        shape((rows, rank)),
        shape((rows, rank)),
    ]
    if grouped:
        outs += [shape((8, 288, rank), F32), shape((8, 288, rank))]
        scratch = [
            pltpu.VMEM((inner + wide, rank), F32),
            pltpu.VMEM((8, 48, half), BF16),
            pltpu.SemaphoreType.DMA((8,)),
        ]
    else:
        outs += [shape((inner, rank), F32), shape((wide, rank), F32)]
        scratch = [pltpu.SemaphoreType.DMA((2,))]
    down, up, act, act_grad, first_term, second_term = call(
        functools.partial(adapter_kernel, grouped, scale),
        (*adapters, attn, cot, hint),
        outs,
        [ANY] * len(adapters) + [VMEM] * 3,
        scratch,
        8.73854,
        18,
    )
    def backward(numbers, near, far):
        count = len(numbers)
        return call(
            functools.partial(backward_kernel, grouped, numbers),
            (q, ko, kf, kt, vo, vf, vt, attn, near, far, act_grad, down),
            [
                shape((rows, count * width)),
                shape((2, rows, count * width), F32),
                shape((2, rows, count * width)),
            ],
            [HBM, HBM, ANY, HBM, HBM, ANY, HBM, ANY] + [VMEM] * 3 + [ANY],
            [
                pltpu.VMEM((count, rows, width), BF16),
                pltpu.VMEM((count, 3 * rows, width), BF16),
                pltpu.VMEM((count, 3 * rows, width), BF16),
                pltpu.VMEM((count, rows, width), BF16),
                pltpu.VMEM((count, width, rank), BF16),
                pltpu.SemaphoreType.DMA((count, 9)),
            ],
            (43.2055, 43.2055, 32.5195, 0.0437518)[numbers[-1]],
            16,
        )

    groups = ((0, 1), (2,), (3,))
    near, far, total = project((1,), pieces[2:4], near, far, total)
    far = swap(far, "seq", 1)
    if grouped:
        term = first_term + swap(second_term, "seq", 1).astype(F32)
        for mask in (2, 1):
            keep = term.shape[0] // 2
            term = term[:keep] + swap(term[keep:].astype(BF16), "fsdp", mask).astype(F32)
        term_far = swap(term[1].astype(BF16), "fsdp", 4)
    dq_a, own_a, away_a = backward(groups[0], near, far)
    away_a = swap(away_a, "seq", 1)
    if grouped:
        pieces[5], pieces[7], near = lax.optimization_barrier((pieces[5], pieces[7], near))
    near_b, far_b, total = project((2,), pieces[4:6], total)
    far_b = swap(far_b, "seq", 1)
    near_c, far_c, own_update, away_update = project((3,), pieces[6:8], total)
    far_c = swap(far_c, "seq", 1)
    away_update = swap(away_update, "seq", 1)
    if grouped:
        near_b, dq_a = lax.optimization_barrier((near_b, dq_a))
    dq_b, own_b, away_b = backward(groups[1], near_b, far_b)
    away_b = swap(away_b, "seq", 1)
    near_c, dq_b = lax.optimization_barrier((near_c, dq_b))
    dq_c, own_c, away_c = backward(groups[2], near_c, far_c)
    away_c = swap(away_c, "seq", 1)
    if not grouped:
        down_grad = lax.psum_scatter(first_term, ("fsdp", "seq"), scatter_dimension=0, tiled=True)
        up_grad = lax.psum_scatter(second_term, ("fsdp", "seq"), scatter_dimension=0, tiled=True).T
    args = [own_update, away_update, act, up]
    outs = [shape((rows, wide))]
    if grouped:
        args += [term, term_far]
        outs += [shape((96, rank), F32), shape((192, rank), F32)]
    update, *adapter_grads = call(
        update_kernel, tuple(args), outs, [VMEM] * len(args), [], 7.44686, 18
    )
    if grouped:
        down_grad, up_grad = adapter_grads[0], adapter_grads[1].T
    args = (dq_a, dq_b, dq_c, own_a, own_b, own_c, away_a, away_b, away_c)
    query_grad, key_grad, value_grad = call(
        functools.partial(finish_kernel, grouped, groups),
        args,
        [shape((rows, inner))] * 3,
        [VMEM] * len(args),
        [],
        44.0671,
        18,
    )
    return (update[None], query_grad[None], key_grad[None], value_grad[None], down_grad, up_grad)


def solution(mesh):
    rows = P(("rep", "fsdp"), "seq", None)
    text = P(("rep", "fsdp"), None, None)
    return jax.shard_map(
        local,
        mesh=mesh,
        in_specs=(
            rows,
            rows,
            rows,
            text,
            text,
            rows,
            P("fsdp", "seq"),
            P("fsdp", None),
            P(None, "fsdp"),
            rows,
        ),
        out_specs=(rows, rows, rows, rows, P(("rep", "fsdp", "seq"), None), P("rep", ("fsdp", "seq"))),
        check_vma=False,
    )
```
